512 devices in a mesh: ctx: 128 (over z, x, core), tp: 4 (over y).
Axes of the slice: x: 4, y: 4, z: 16, core: 2. Of those that a mesh axis runs over, the one named last changes fastest.
Arguments:
- queries: bfloat16 [32768, 2048], P('ctx', 'tp'), may hold values from -8 to 8
- key_proj: bfloat16 [32768, 2048], P('ctx', 'tp'), may hold values from -8 to 8
- value_proj: bfloat16 [32768, 2048], P('ctx', 'tp'), may hold values from -4 to 4
- router: bfloat16 [32768], P('ctx'), may hold values from 0.5 to 2
- chosen: int32 [16, 256], replicated, may hold values from 0 to 32767, as said below
- out_weight: bfloat16 [2048, 4096], P('tp'), may hold values from -0.125 to 0.125
Outputs:
- update: bfloat16 [32768, 4096], P('ctx', 'tp')
The draws below stay inside these ranges and needn't reach their ends.
Inputs may be any that keep to these rules, and one draw needn't show every extreme that they name: `chosen`: row b holds 256 ascending positions of b * 2048 to b * 2048 + 2047. Each run of 128 positions that starts at a multiple of 128 holds at most 32 of them, and in every row one such run holds exactly 32.
All inputs are finite; a program needn't handle non-finite values.
Results may differ from the reference program's by a relative error of at most 0.017.
Values may be sent and summed in bfloat16 or wider, within the bound.
A program may use at most 128 MiB of HBM per device.

```python
import math
import jax
import jax.numpy as jnp
from jax import lax

D = 4096
HEADS = 16
HD = 128
TOK_DEV = 256
TOKENS = 32768
PIECE = 128
BLOCK = 2048
PICK = 256
BLOCKS = 16
N_CTX = 128


def drawn_rows(key):
    drawn = jnp.clip(jax.random.normal(key, (TOKENS, HEADS * HD)), -4.0, 4.0)
    return drawn.astype(jnp.bfloat16)


def draw_queries(key, part):
    key = jax.random.fold_in(key, 11)
    return drawn_rows(key)


def draw_key_proj(key, part):
    key = jax.random.fold_in(key, 12)
    return drawn_rows(key)


def permute_piece(piece_key):
    return jax.random.permutation(piece_key, PIECE)


def draw_chosen(key, part):
    key = jax.random.fold_in(key, 13)
    per_block = BLOCK // PIECE
    step_size = PIECE // 16

    def one_block(block_key, block_index):
        keys_all = jax.random.split(block_key, 5)
        first_order = jax.random.permutation(keys_all[0], per_block)
        second_order = jax.random.permutation(keys_all[1], per_block)
        shift_one = jax.random.randint(keys_all[2], (per_block // 2,), -step_size, step_size + 1)
        shift_two = jax.random.randint(keys_all[3], (per_block // 2,), -step_size, step_size + 1)
        shift_one = shift_one.at[0].set(step_size)
        star_at = jnp.argmax((second_order == first_order[0]).astype(jnp.int32))
        shift_two = shift_two.at[star_at // 2].set(jnp.where(star_at % 2 == 0, step_size, -step_size))
        alternate = jnp.tile(jnp.array([1, -1], jnp.int32), per_block // 2)
        counts = jnp.full((per_block,), PIECE // 8, jnp.int32)
        counts = counts.at[first_order].add(jnp.repeat(shift_one, 2) * alternate)
        counts = counts.at[second_order].add(jnp.repeat(shift_two, 2) * alternate)
        ranks = jax.vmap(permute_piece)(jax.random.split(keys_all[4], per_block))
        picked = (ranks < counts[:, None]).reshape(-1).astype(jnp.int32)
        offsets = jnp.argsort(1 - picked, stable=True)[:PICK]
        return (offsets + block_index * BLOCK).astype(jnp.int32)
    return jax.vmap(one_block)(jax.random.split(key, BLOCKS), jnp.arange(BLOCKS, dtype=jnp.int32))


def block_levels(stream_key, shape, cuts, smallest, largest):
    def one(dim, parts):
        steps = jax.random.uniform(jax.random.fold_in(jax.random.fold_in(stream_key, 6), dim), (parts,), jnp.float32, smallest / len(cuts), largest / len(cuts))
        return jnp.repeat(jnp.exp(steps), shape[dim] // parts).reshape((-1,) + (1,) * (len(shape) - dim - 1))

    factor_of = one(*cuts[0])
    for cut in cuts[1:]:
        factor_of = factor_of * one(*cut)
    return factor_of


def bell_draw(key, dims, spread, most, shards=(), kind=jnp.bfloat16):
    gain = block_levels(key, dims, shards, -0.22, 0.18) if shards else 1.0
    values = jax.random.normal(key, dims, jnp.float32) * spread * gain
    return jnp.minimum(jnp.maximum(values, -most), most).astype(kind)


def setup_inputs(seed: int = 0) -> dict:
    splits = jax.random.split(jax.random.key(seed), 7)
    return {
        "queries": draw_queries(jax.random.fold_in(splits[6], 71), 0),
        "key_proj": draw_key_proj(jax.random.fold_in(splits[6], 71), 0),
        "value_proj": bell_draw(splits[2], (TOKENS, HEADS * HD), 1.0, 4.0, ((0, 128), (1, 4))),
        "router": jnp.clip(jnp.exp(math.log(2.0) - 1.3862944 * jax.random.uniform(splits[3], (TOKENS,), jnp.float32) ** block_levels(splits[3], (TOKENS,), ((0, 128),), -0.2, 0.2)), 0.5, 2.0).astype(jnp.bfloat16),
        "chosen": draw_chosen(jax.random.fold_in(splits[6], 71), 0),
        "out_weight": bell_draw(splits[5], (HEADS * HD, D), (HEADS * HD) ** -0.5, 0.125, ((0, 4),)),
    }


def storage_rows(positions):
    piece_id = positions // PIECE
    offset = positions % PIECE
    second = piece_id >= N_CTX
    device = jnp.where(second, 2 * N_CTX - 1 - piece_id, piece_id)
    return (device * TOK_DEV + second.astype(jnp.int32) * PIECE + offset).astype(jnp.int32)


def reference(queries, key_proj, value_proj, router, chosen, out_weight):
    positions = chosen.reshape(-1).astype(jnp.int32)
    rows = storage_rows(positions)
    picked_query = queries[rows]
    picked_key = key_proj[rows]
    picked_value = value_proj[rows]
    allowed = positions[None, :] <= positions[:, None]

    def one_head(head):
        first_col = (head * HD).astype(jnp.int32)
        query_head = lax.dynamic_slice_in_dim(picked_query, first_col, HD, 1)
        key_head = lax.dynamic_slice_in_dim(picked_key, first_col, HD, 1)
        value_head = lax.dynamic_slice_in_dim(picked_value, first_col, HD, 1)
        scores = jnp.dot(query_head, key_head.T, preferred_element_type=jnp.float32) * (HD ** -0.5)
        masked = jnp.where(allowed, scores, -jnp.inf)
        top = jnp.max(masked, axis=1, keepdims=True)
        weights = jnp.where(allowed, jnp.exp(masked - top), 0.0)
        totals = jnp.sum(weights, axis=1, keepdims=True)
        summed = jnp.dot(weights.astype(jnp.bfloat16), value_head, preferred_element_type=jnp.float32)
        return summed / totals

    per_head = lax.map(one_head, jnp.arange(HEADS, dtype=jnp.int32))
    attended = jnp.transpose(per_head, (1, 0, 2)).reshape(positions.shape[0], HEADS * HD).astype(jnp.bfloat16)
    projected = jnp.dot(attended, out_weight, preferred_element_type=jnp.float32)
    updates = (projected * router[rows].astype(jnp.float32)[:, None]).astype(jnp.bfloat16)
    return jnp.zeros((TOKENS, D), jnp.bfloat16).at[rows].set(updates)
```

```python
import functools
import jax
import jax.numpy as jnp
from jax import lax
from jax.experimental import pallas as pl
from jax.experimental.pallas import tpu as pltpu
from jax.sharding import PartitionSpec as P

HD = 128
PIECE = 128
MOST = 32
PICK = 256
GROUP = 16
CHIPS = 8
RING = 16
SUBS = 4
SUB = PICK // SUBS
MESH = pl.DeviceIdType.MESH
F32 = jnp.float32
BF16 = jnp.bfloat16


def one_hots(chosen_row, base):
    first = jnp.sum((chosen_row < base).astype(jnp.int32), axis=1, keepdims=True)
    inside = (chosen_row >= base) & (chosen_row < base + PIECE)
    entry = lax.broadcasted_iota(jnp.int32, (MOST, PICK), 1)
    rank = lax.broadcasted_iota(jnp.int32, (MOST, PICK), 0)
    by_rank = (entry - first == rank) & inside
    token = lax.broadcasted_iota(jnp.int32, (PIECE, PICK), 0)
    by_token = chosen_row - base == token
    return by_rank.astype(F32).astype(BF16), by_token.astype(F32).astype(BF16)


def dot_nt(a, b):
    return lax.dot_general(a, b, (((1,), (1,)), ((), ())), preferred_element_type=F32)


def body(
    q_ref, k_ref, v_ref, router_ref, chosen_ref, w_hbm, out_ref,
    sel, kvpad, qpad, kv, att, osend, wbuf, place, rsel, top, total, acc, pick,
    s1, r1_kv, r1_q, s2, r2_right, r2_left, s_sib, r_sib, s3, r3, s_w, r_w, s_wf, r_wf, l_w,
):
    ctx = lax.axis_index("ctx")
    y = lax.axis_index("tp")
    z = ctx // 8
    core = ctx % 2
    x = (ctx // 2) % 4
    group = ctx // GROUP
    chip = (ctx // 2) % CHIPS
    half = z % 2
    block = half * (15 - 2 * group) + group

    def ctx_of(chip_to, core_to):
        return group * GROUP + chip_to * 2 + core_to

    def ctx_at(z_to, core_to):
        return z_to * 8 + x * 2 + core_to

    sibling = ctx_of(chip, 1 - core)
    z_right = (z + 1) % RING
    z_left = (z + RING - 1) % RING

    barrier = pltpu.get_barrier_semaphore()

    def greet(ctx_to, y_to):
        pl.semaphore_signal(barrier, inc=1, device_id=(ctx_to, y_to), device_id_type=MESH)

    def greet_chip(r, carry):
        chip_to = (chip + r) % CHIPS
        greet(ctx_of(chip_to, core), y)
        greet(ctx_of(chip_to, core), (y + 1) % 4)
        greet(ctx_of(chip_to, core), (y + 2) % 4)
        greet(ctx_of(chip_to, core), (y + 3) % 4)
        greet(ctx_of(chip_to, 1 - core), y)
        return carry

    lax.fori_loop(1, CHIPS, greet_chip, 0)
    greet(sibling, y)
    for step in range(1, 4):
        greet(ctx, (y + step) % 4)
    z_far = (z + half * 2 - 1 + RING) % RING
    greet(ctx_at(z_far, core), y)

    w_rows = w_hbm.shape[0]
    w_cols = wbuf.shape[1]
    half_rows = w_rows // 2
    own_w = pltpu.make_async_copy(
        w_hbm.at[:, pl.ds(pl.multiple_of(y * w_cols, w_cols), w_cols)],
        wbuf.at[pl.ds(pl.multiple_of(y * w_rows, w_rows), w_rows), :],
        l_w,
    )
    own_w.start()

    for hf in range(2):
        piece = ctx if hf == 0 else 255 - ctx
        row = chosen_ref[pl.ds(piece // GROUP, 1), :]
        by_rank, by_token = one_hots(row, piece * PIECE)
        picks = dot_nt(by_rank, by_token)
        pick_bf = picks.astype(BF16)
        place[hf] = dot_nt(by_token, by_rank).astype(BF16)
        rows = slice(hf * PIECE, (hf + 1) * PIECE)
        rsel[hf * MOST : (hf + 1) * MOST, :] = jnp.sum(
            picks * router_ref[:, rows].astype(F32), axis=1, keepdims=True
        )
        for kind, ref in enumerate((k_ref, v_ref, q_ref)):
            picked = jnp.dot(pick_bf, ref[rows, :], preferred_element_type=F32).astype(BF16)
            for head in range(4):
                sel[kind, hf * 4 + head] = picked[:, head * HD : (head + 1) * HD]

    pl.semaphore_wait(barrier, 40)

    my_rows = pl.ds(pl.multiple_of((chip * 2 + core) * MOST, MOST), MOST)
    my_q_rows = pl.ds(pl.multiple_of(chip * MOST, MOST), MOST)

    def first_kv(chip_to, core_to):
        return pltpu.make_async_remote_copy(
            src_ref=sel.at[core_to, chip_to],
            dst_ref=kvpad.at[my_rows, :],
            send_sem=s1, recv_sem=r1_kv,
            device_id=(ctx_of(chip_to, core_to), y), device_id_type=MESH,
        )

    def first_q(chip_to):
        return pltpu.make_async_remote_copy(
            src_ref=sel.at[2, chip_to],
            dst_ref=qpad.at[my_q_rows, :],
            send_sem=s1, recv_sem=r1_q,
            device_id=(ctx_of(chip_to, core), y), device_id_type=MESH,
        )

    first_kv(chip, 1 - core).start()

    def first_sends(r, carry):
        chip_to = (chip + r) % CHIPS
        first_kv(chip_to, core).start()
        first_kv(chip_to, 1 - core).start()
        first_q(chip_to).start()
        return carry

    lax.fori_loop(1, CHIPS, first_sends, 0)
    kvpad[my_rows, :] = sel[core, chip]
    qpad[my_q_rows, :] = sel[2, chip]

    def weights(step):
        y_to = (y + step) % 4
        return pltpu.make_async_remote_copy(
            src_ref=w_hbm.at[
                pl.ds(pl.multiple_of(core * half_rows, half_rows), half_rows),
                pl.ds(pl.multiple_of(y_to * w_cols, w_cols), w_cols),
            ],
            dst_ref=wbuf.at[
                pl.ds(pl.multiple_of(y * w_rows + core * half_rows, half_rows), half_rows), :
            ],
            send_sem=s_w, recv_sem=r_w.at[step - 1],
            device_id=(ctx, y_to), device_id_type=MESH,
        )

    for step in (1, 3, 2):
        weights(step).start()

    row = chosen_ref[pl.ds(block, 1), :]
    diagonal = lax.broadcasted_iota(jnp.int32, (PICK, PICK), 0) == lax.broadcasted_iota(
        jnp.int32, (PICK, PICK), 1
    )
    column = jnp.sum(jnp.where(diagonal, row, 0), axis=1, keepdims=True)

    def base_of(device):
        return block * 2048 + (half * 15 + (1 - 2 * half) * device) * PIECE

    slot = lax.broadcasted_iota(jnp.int32, (1, GROUP * MOST), 1)
    base = base_of(slot // MOST)
    first = jnp.sum((column < base).astype(jnp.int32), axis=0, keepdims=True)
    inside = (column >= base) & (column < base + PIECE)
    entry = lax.broadcasted_iota(jnp.int32, (PICK, GROUP * MOST), 0)
    pick[...] = ((entry - first == slot % MOST) & inside).astype(F32).astype(BF16)
    q_slot = lax.broadcasted_iota(jnp.int32, (CHIPS * MOST, 1), 0)
    q_base = base_of(q_slot // MOST * 2 + core)
    q_place = jnp.sum((row < q_base).astype(jnp.int32), axis=1, keepdims=True) + q_slot % MOST

    pltpu.make_async_copy(kv.at[pl.ds(0, 15 * MOST), :], kv.at[pl.ds(0, 15 * MOST), :], r1_kv).wait()

    def rows_of(kind, z_from, sub=None):
        if sub is None:
            return pl.ds(pl.multiple_of((kind * RING + z_from) * PICK, PICK), PICK)
        return pl.ds(pl.multiple_of((kind * RING + z_from) * PICK + sub * SUB, SUB), SUB)

    kv[rows_of(core, z), :] = jnp.dot(
        pick[...], kvpad[...], preferred_element_type=F32
    ).astype(BF16)

    def to_right(z_from, sub, step):
        rows = rows_of(core, z_from, sub)
        return pltpu.make_async_remote_copy(
            src_ref=kv.at[rows, :], dst_ref=kv.at[rows, :],
            send_sem=s2, recv_sem=r2_right.at[step * SUBS + sub],
            device_id=(ctx_at(z_right, core), y), device_id_type=MESH,
        )

    def to_left(z_from, sub, step):
        rows = rows_of(core, z_from, sub)
        return pltpu.make_async_remote_copy(
            src_ref=kv.at[rows, :], dst_ref=kv.at[rows, :],
            send_sem=s2, recv_sem=r2_left.at[step * SUBS + sub],
            device_id=(ctx_at(z_left, core), y), device_id_type=MESH,
        )

    def to_sibling(z_from):
        rows = rows_of(core, z_from)
        return pltpu.make_async_remote_copy(
            src_ref=kv.at[rows, :], dst_ref=kv.at[rows, :],
            send_sem=s_sib, recv_sem=r_sib.at[z_from],
            device_id=(sibling, y), device_id_type=MESH,
        )

    for sub in range(SUBS):
        to_right(z, sub, 0).start()
        to_left(z, sub, 0).start()
    to_sibling(z).start()

    pltpu.make_async_copy(kv.at[pl.ds(0, 7 * MOST), :], kv.at[pl.ds(0, 7 * MOST), :], r1_q).wait()

    scale = HD**-0.5 * 1.4426950408889634

    def from_sibling(z_from):
        rows = rows_of(1 - core, z_from)
        pltpu.make_async_copy(kv.at[rows, :], kv.at[rows, :], r_sib.at[z_from]).wait()

    def attend_own():
        from_sibling(z)
        scores = dot_nt(qpad[...], kv[rows_of(0, z), :]) * scale
        seen = lax.broadcasted_iota(jnp.int32, (PICK, PICK), 1) <= q_place
        scores = jnp.where(seen, scores, -1e30)
        top_now = jnp.max(scores, axis=1, keepdims=True)
        weight = jnp.exp2(scores - top_now)
        top[...] = top_now
        total[...] = jnp.sum(weight, axis=1, keepdims=True)
        acc[...] = jnp.dot(weight.astype(BF16), kv[rows_of(1, z), :], preferred_element_type=F32)

    def attend(z_from):
        from_sibling(z_from)
        half_from = z_from % 2
        block_from = half_from * 15 + (1 - 2 * half_from) * (z_from // 2)

        @pl.when(block_from < block)
        def _():
            scores = dot_nt(qpad[...], kv[rows_of(0, z_from), :]) * scale
            top_was = top[...]
            top_now = jnp.maximum(top_was, jnp.max(scores, axis=1, keepdims=True))
            weight = jnp.exp2(scores - top_now)
            fade = jnp.exp2(top_was - top_now)
            top[...] = top_now
            total[...] = total[...] * fade + jnp.sum(weight, axis=1, keepdims=True)
            acc[...] = acc[...] * fade + jnp.dot(
                weight.astype(BF16), kv[rows_of(1, z_from), :], preferred_element_type=F32
            )

    def ring_step(step, carry):
        from_left = (z + RING - step) % RING
        from_right = (z + step) % RING
        for sub in range(SUBS):
            rows = rows_of(core, from_left, sub)
            pltpu.make_async_copy(
                kv.at[rows, :], kv.at[rows, :], r2_right.at[(step - 1) * SUBS + sub]
            ).wait()
            if sub < SUBS // 2:
                to_right(from_left, sub, step).start()
            else:

                @pl.when(step < 7)
                def _():
                    to_right(from_left, sub, step).start()

            rows = rows_of(core, from_right, sub)
            pltpu.make_async_copy(
                kv.at[rows, :], kv.at[rows, :], r2_left.at[(step - 1) * SUBS + sub]
            ).wait()
            if sub >= SUBS // 2:
                to_left(from_right, sub, step).start()
            else:

                @pl.when(step < 7)
                def _():
                    to_left(from_right, sub, step).start()

        to_sibling(from_left).start()
        to_sibling(from_right).start()

        @pl.when(step == 1)
        def _():
            attend_own()

        @pl.when(step > 1)
        def _():
            attend((z + RING - step + 1) % RING)
            attend((z + step - 1) % RING)

        return carry

    lax.fori_loop(1, 8, ring_step, 0)
    z_last = (z + 8) % RING
    for sub in range(SUBS):
        rows = rows_of(core, z_last, sub)
        sem = r2_right if sub < SUBS // 2 else r2_left
        pltpu.make_async_copy(kv.at[rows, :], kv.at[rows, :], sem.at[7 * SUBS + sub]).wait()
    to_sibling(z_last).start()
    attend((z + RING - 7) % RING)
    attend((z + 7) % RING)
    attend(z_last)

    osend[...] = (acc[...] / total[...]).astype(BF16)

    att_rows = pl.ds(pl.multiple_of(half * MOST, MOST), MOST)
    att_cols = pl.ds(pl.multiple_of((y * 4 + x) * HD, HD), HD)

    def back(chip_to, y_to):
        return pltpu.make_async_remote_copy(
            src_ref=osend.at[pl.ds(pl.multiple_of(chip_to * MOST, MOST), MOST), :],
            dst_ref=att.at[att_rows, att_cols],
            send_sem=s3, recv_sem=r3,
            device_id=(ctx_of(chip_to, core), y_to), device_id_type=MESH,
        )

    for step in range(1, 4):
        back(chip, (y + step) % 4).start()

    def backs(r, carry):
        chip_to = (chip + r) % CHIPS
        for step in range(4):
            back(chip_to, (y + step) % 4).start()
        return carry

    lax.fori_loop(1, CHIPS, backs, 0)
    att[att_rows, att_cols] = osend[my_q_rows, :]

    def pass_on(step):
        y_from = (y + 4 - step) % 4
        rows = pl.ds(pl.multiple_of(y_from * w_rows + core * half_rows, half_rows), half_rows)
        pltpu.make_async_copy(wbuf.at[rows, :], wbuf.at[rows, :], r_w.at[step - 1]).wait()
        pltpu.make_async_remote_copy(
            src_ref=wbuf.at[rows, :], dst_ref=wbuf.at[rows, :],
            send_sem=s_wf, recv_sem=r_wf,
            device_id=(sibling, y), device_id_type=MESH,
        ).start()

    for step in (1, 3, 2):
        pass_on(step)
    own_w.wait()
    three = wbuf.at[pl.ds(0, 3 * half_rows), :]
    pltpu.make_async_copy(three, three, r_wf).wait()
    pltpu.make_async_copy(kv.at[pl.ds(0, 31 * MOST), :], kv.at[pl.ds(0, 31 * MOST), :], r3).wait()

    updates = jnp.dot(att[...], wbuf[...], preferred_element_type=F32) * rsel[...]
    updates = updates.astype(BF16)
    for hf in range(2):
        out_ref[hf * PIECE : (hf + 1) * PIECE, :] = jnp.dot(
            place[hf], updates[hf * MOST : (hf + 1) * MOST, :], preferred_element_type=F32
        ).astype(BF16)

    sent = kv.at[pl.ds(0, 22 * MOST), :]
    pltpu.make_async_copy(sent, sent, s1).wait()
    sent = kv.at[pl.ds(0, 15 * PICK), :]
    pltpu.make_async_copy(sent, sent, s2).wait()
    sent = kv.at[pl.ds(0, 16 * PICK), :]
    pltpu.make_async_copy(sent, sent, s_sib).wait()
    sent = kv.at[pl.ds(0, 31 * MOST), :]
    pltpu.make_async_copy(sent, sent, s3).wait()
    pltpu.make_async_copy(three, three, s_w).wait()
    pltpu.make_async_copy(three, three, s_wf).wait()


def shards(queries, key_proj, value_proj, router, chosen, out_weight):
    tok_rows = queries.shape[0]
    w_cols = out_weight.shape[1] // 4
    dma = pltpu.SemaphoreType.DMA
    vmem = pl.BlockSpec(memory_space=pltpu.VMEM)
    return pl.pallas_call(
        body,
        out_shape=jax.ShapeDtypeStruct((tok_rows, w_cols), BF16),
        in_specs=[vmem] * 5 + [pl.BlockSpec(memory_space=pl.ANY)],
        out_specs=vmem,
        scratch_shapes=[
            pltpu.VMEM((3, CHIPS, MOST, HD), BF16),
            pltpu.VMEM((GROUP * MOST, HD), BF16),
            pltpu.VMEM((CHIPS * MOST, HD), BF16),
            pltpu.VMEM((2 * RING * PICK, HD), BF16),
            pltpu.VMEM((2 * MOST, 16 * HD), BF16),
            pltpu.VMEM((CHIPS * MOST, HD), BF16),
            pltpu.VMEM((4 * out_weight.shape[0], w_cols), BF16),
            pltpu.VMEM((2, PIECE, MOST), BF16),
            pltpu.VMEM((2 * MOST, 1), F32),
            pltpu.VMEM((CHIPS * MOST, 1), F32),
            pltpu.VMEM((CHIPS * MOST, 1), F32),
            pltpu.VMEM((CHIPS * MOST, HD), F32),
            pltpu.VMEM((PICK, GROUP * MOST), BF16),
            dma, dma, dma,
            dma, dma((8 * SUBS,)), dma((8 * SUBS,)),
            dma, dma((RING,)),
            dma, dma,
            dma, dma((3,)), dma, dma, dma,
        ],
        compiler_params=pltpu.CompilerParams(
            collective_id=0, has_side_effects=True, vmem_limit_bytes=40 * 1024 * 1024
        ),
        name="routed_attention",
    )(queries, key_proj, value_proj, router.reshape(1, tok_rows), chosen, out_weight)


def solution(mesh):
    placed = (P("ctx", "tp"), P("ctx", "tp"), P("ctx", "tp"), P("ctx"), P(), P("tp", None))
    return jax.shard_map(
        shards, mesh=mesh, in_specs=placed, out_specs=P("ctx", "tp"), check_vma=False
    )
```

```python
import functools
import jax
import jax.numpy as jnp
from jax import lax
from jax.experimental import pallas as pl
from jax.experimental.pallas import tpu as pltpu
from jax.sharding import PartitionSpec as P

HD = 128
PIECE = 128
MOST = 32
PICK = 256
GROUP = 16
CHIPS = 8
RING = 16
SUBS = 2
SUB = PICK // SUBS
MESH = pl.DeviceIdType.MESH
F32 = jnp.float32
BF16 = jnp.bfloat16


def one_hots(chosen_row, base):
    first = jnp.sum((chosen_row < base).astype(jnp.int32), axis=1, keepdims=True)
    inside = (chosen_row >= base) & (chosen_row < base + PIECE)
    entry = lax.broadcasted_iota(jnp.int32, (MOST, PICK), 1)
    rank = lax.broadcasted_iota(jnp.int32, (MOST, PICK), 0)
    by_rank = (entry - first == rank) & inside
    token = lax.broadcasted_iota(jnp.int32, (PIECE, PICK), 0)
    by_token = chosen_row - base == token
    return by_rank.astype(F32).astype(BF16), by_token.astype(F32).astype(BF16)


def dot_nt(a, b):
    return lax.dot_general(a, b, (((1,), (1,)), ((), ())), preferred_element_type=F32)


def body(
    q_hbm, k_hbm, v_hbm, router_ref, chosen_hbm, w_hbm, out_ref,
    q_ref, k_ref, v_ref, chosen_ref, l_in, sel, pad_own, pad_other, kv, att, osend, wbuf, place, rsel, top, total, acc, pick,
    s1, r1_own, r1_other, s2, r2_far_right, r2_far_left, r2_near_right, r2_near_left, s_sib, r_sib, s3, r3, s_w, r_w, s_wf, r_wf, l_w,
):
    ctx = lax.axis_index("ctx")
    y = lax.axis_index("tp")
    z = ctx // 8
    core = ctx % 2
    x = (ctx // 2) % 4
    group = ctx // GROUP
    chip = (ctx // 2) % CHIPS
    half = z % 2
    block = half * (15 - 2 * group) + group

    def ctx_of(chip_to, core_to):
        return group * GROUP + chip_to * 2 + core_to

    def ctx_at(z_to, core_to):
        return z_to * 8 + x * 2 + core_to

    sibling = ctx_of(chip, 1 - core)
    z_right = (z + 1) % RING
    z_left = (z + RING - 1) % RING

    loads = [
        pltpu.make_async_copy(src, dst, l_in.at[n])
        for n, (src, dst) in enumerate(
            ((chosen_hbm, chosen_ref), (k_hbm, k_ref), (v_hbm, v_ref), (q_hbm, q_ref))
        )
    ]
    for load in loads:
        load.start()

    barrier = pltpu.get_barrier_semaphore()

    def greet(ctx_to, y_to):
        pl.semaphore_signal(barrier, inc=1, device_id=(ctx_to, y_to), device_id_type=MESH)

    def greet_chip(r, carry):
        chip_to = (chip + r) % CHIPS
        greet(ctx_of(chip_to, core), y)
        greet(ctx_of(chip_to, 1 - core), y)
        return carry

    lax.fori_loop(1, CHIPS, greet_chip, 0)
    greet(sibling, y)
    for step in range(1, 4):
        greet(ctx, (y + step) % 4)
    greet(ctx_at((z + half * 2 - 1 + RING) % RING, core), y)
    greet(ctx_at((z + 2) % RING, core), y)
    greet(ctx_at((z + RING - 2) % RING, core), y)

    w_rows = w_hbm.shape[0]
    w_cols = wbuf.shape[1]
    half_rows = w_rows // 2
    own_w = pltpu.make_async_copy(
        w_hbm.at[:, pl.ds(pl.multiple_of(y * w_cols, w_cols), w_cols)],
        wbuf.at[pl.ds(pl.multiple_of(y * w_rows, w_rows), w_rows), :],
        l_w,
    )
    own_w.start()

    for load in loads:
        load.wait()

    for hf in range(2):
        piece = ctx if hf == 0 else 255 - ctx
        row = chosen_ref[pl.ds(piece // GROUP, 1), :]
        by_rank, by_token = one_hots(row, piece * PIECE)
        picks = dot_nt(by_rank, by_token)
        pick_bf = picks.astype(BF16)
        place[hf] = dot_nt(by_token, by_rank).astype(BF16)
        rows = slice(hf * PIECE, (hf + 1) * PIECE)
        rsel[hf * MOST : (hf + 1) * MOST, :] = jnp.sum(
            picks * router_ref[:, rows].astype(F32), axis=1, keepdims=True
        )
        for kind, ref in ((1 - core, k_ref), (core, v_ref), (2, q_ref)):
            picked = jnp.dot(pick_bf, ref[rows, :], preferred_element_type=F32).astype(BF16)
            for head in range(4):
                sel[hf * 4 + head, kind] = picked[:, head * HD : (head + 1) * HD]

    pl.semaphore_wait(barrier, 21)

    my_q_rows = pl.ds(pl.multiple_of(chip * MOST, MOST), MOST)

    def first_own(chip_to):
        return pltpu.make_async_remote_copy(
            src_ref=sel.at[chip_to, pl.ds(1, 2)],
            dst_ref=pad_own.at[chip],
            send_sem=s1, recv_sem=r1_own,
            device_id=(ctx_of(chip_to, core), y), device_id_type=MESH,
        )

    def first_other(chip_to):
        return pltpu.make_async_remote_copy(
            src_ref=sel.at[chip_to, 0],
            dst_ref=pad_other.at[chip],
            send_sem=s1, recv_sem=r1_other,
            device_id=(ctx_of(chip_to, 1 - core), y), device_id_type=MESH,
        )

    def first_sends(r, carry):
        chip_to = (chip + r) % CHIPS
        first_own(chip_to).start()
        first_other(chip_to).start()
        return carry

    lax.fori_loop(1, CHIPS, first_sends, 0)
    first_other(chip).start()
    pad_own[chip] = sel[chip, 1:3]

    def weights(step):
        y_to = (y + step) % 4
        return pltpu.make_async_remote_copy(
            src_ref=w_hbm.at[
                pl.ds(pl.multiple_of(core * half_rows, half_rows), half_rows),
                pl.ds(pl.multiple_of(y_to * w_cols, w_cols), w_cols),
            ],
            dst_ref=wbuf.at[
                pl.ds(pl.multiple_of(y * w_rows + core * half_rows, half_rows), half_rows), :
            ],
            send_sem=s_w, recv_sem=r_w.at[step - 1],
            device_id=(ctx, y_to), device_id_type=MESH,
        )

    for step in (1, 3, 2):
        weights(step).start()

    row = chosen_ref[pl.ds(block, 1), :]
    diagonal = lax.broadcasted_iota(jnp.int32, (PICK, PICK), 0) == lax.broadcasted_iota(
        jnp.int32, (PICK, PICK), 1
    )
    column = jnp.sum(jnp.where(diagonal, row, 0), axis=1, keepdims=True)

    def base_of(device):
        return block * 2048 + (half * 15 + (1 - 2 * half) * device) * PIECE

    slot = lax.broadcasted_iota(jnp.int32, (1, GROUP * MOST), 1)
    slot_core = (core + slot // (CHIPS * MOST)) % 2
    base = base_of(slot // MOST % CHIPS * 2 + slot_core)
    first = jnp.sum((column < base).astype(jnp.int32), axis=0, keepdims=True)
    inside = (column >= base) & (column < base + PIECE)
    entry = lax.broadcasted_iota(jnp.int32, (PICK, GROUP * MOST), 0)
    pick[...] = ((entry - first == slot % MOST) & inside).astype(F32).astype(BF16)
    q_slot = lax.broadcasted_iota(jnp.int32, (CHIPS * MOST, 1), 0)
    q_base = base_of(q_slot // MOST * 2 + core)
    q_place = jnp.sum((row < q_base).astype(jnp.int32), axis=1, keepdims=True) + q_slot % MOST

    arrived = pad_own.at[pl.ds(0, CHIPS - 1)]
    pltpu.make_async_copy(arrived, arrived, r1_own).wait()
    pltpu.make_async_copy(pad_other, pad_other, r1_other).wait()

    def rows_of(kind, z_from, sub=None):
        if sub is None:
            return pl.ds(pl.multiple_of((kind * RING + z_from) * PICK, PICK), PICK)
        return pl.ds(pl.multiple_of((kind * RING + z_from) * PICK + sub * SUB, SUB), SUB)

    own_side = jnp.dot(
        pick[:, : CHIPS * MOST],
        pad_own[:, 0].reshape(CHIPS * MOST, HD),
        preferred_element_type=F32,
    )
    other_side = jnp.dot(
        pick[:, CHIPS * MOST :],
        pad_other[...].reshape(CHIPS * MOST, HD),
        preferred_element_type=F32,
    )
    kv[rows_of(core, z), :] = (own_side + other_side).astype(BF16)

    def carry_on(z_from, sub, level, way, reach, sems):
        rows = rows_of(core, z_from, sub)
        return pltpu.make_async_remote_copy(
            src_ref=kv.at[rows, :], dst_ref=kv.at[rows, :],
            send_sem=s2, recv_sem=sems.at[level * SUBS + sub],
            device_id=(ctx_at((z + RING + way * reach) % RING, core), y), device_id_type=MESH,
        )

    def far(z_from, sub, level, way):
        return carry_on(z_from, sub, level, way, 2, r2_far_right if way > 0 else r2_far_left)

    def near(z_from, sub, level, way):
        return carry_on(z_from, sub, level, way, 1, r2_near_right if way > 0 else r2_near_left)

    def arrive(z_from, sub, level, sems):
        rows = rows_of(core, z_from, sub)
        pltpu.make_async_copy(kv.at[rows, :], kv.at[rows, :], sems.at[level * SUBS + sub]).wait()

    def to_sibling(z_from):
        rows = rows_of(core, z_from)
        return pltpu.make_async_remote_copy(
            src_ref=kv.at[rows, :], dst_ref=kv.at[rows, :],
            send_sem=s_sib, recv_sem=r_sib.at[z_from],
            device_id=(sibling, y), device_id_type=MESH,
        )

    for send in (far, near):
        for sub in range(SUBS):
            send(z, sub, 0, 1).start()
            send(z, sub, 0, -1).start()
    to_sibling(z).start()

    scale = HD**-0.5 * 1.4426950408889634

    def from_sibling(z_from):
        rows = rows_of(1 - core, z_from)
        pltpu.make_async_copy(kv.at[rows, :], kv.at[rows, :], r_sib.at[z_from]).wait()

    def attend_own():
        from_sibling(z)
        scores = dot_nt(pad_own[:, 1].reshape(CHIPS * MOST, HD), kv[rows_of(0, z), :]) * scale
        seen = lax.broadcasted_iota(jnp.int32, (PICK, PICK), 1) <= q_place
        scores = jnp.where(seen, scores, -1e30)
        top_now = jnp.max(scores, axis=1, keepdims=True)
        weight = jnp.exp2(scores - top_now)
        top[...] = top_now
        total[...] = jnp.sum(weight, axis=1, keepdims=True)
        acc[...] = jnp.dot(weight.astype(BF16), kv[rows_of(1, z), :], preferred_element_type=F32)

    def attend(z_from):
        from_sibling(z_from)
        half_from = z_from % 2
        block_from = half_from * 15 + (1 - 2 * half_from) * (z_from // 2)

        @pl.when(block_from < block)
        def _():
            scores = dot_nt(pad_own[:, 1].reshape(CHIPS * MOST, HD), kv[rows_of(0, z_from), :]) * scale
            top_was = top[...]
            top_now = jnp.maximum(top_was, jnp.max(scores, axis=1, keepdims=True))
            weight = jnp.exp2(scores - top_now)
            fade = jnp.exp2(top_was - top_now)
            top[...] = top_now
            total[...] = total[...] * fade + jnp.sum(weight, axis=1, keepdims=True)
            acc[...] = acc[...] * fade + jnp.dot(
                weight.astype(BF16), kv[rows_of(1, z_from), :], preferred_element_type=F32
            )

    def level_step(level, carry):
        from_left = (z + RING - 2 * level) % RING
        from_right = (z + 2 * level) % RING
        for sub in range(SUBS):
            arrive(from_left, sub, level - 1, r2_far_right)
            if sub < SUBS // 2:
                far(from_left, sub, level, 1).start()
            else:

                @pl.when(level < 3)
                def _():
                    far(from_left, sub, level, 1).start()

            arrive(from_right, sub, level - 1, r2_far_left)
            if sub >= SUBS // 2:
                far(from_right, sub, level, -1).start()
            else:

                @pl.when(level < 3)
                def _():
                    far(from_right, sub, level, -1).start()

        for sub in range(SUBS):
            near(from_left, sub, level, 1).start()
            near(from_right, sub, level, -1).start()
        to_sibling(from_left).start()
        to_sibling(from_right).start()
        next_left = (z + RING - 2 * level + 1) % RING
        next_right = (z + 2 * level - 1) % RING
        for sub in range(SUBS):
            arrive(next_left, sub, level - 1, r2_near_right)
            arrive(next_right, sub, level - 1, r2_near_left)
        to_sibling(next_left).start()
        to_sibling(next_right).start()

        @pl.when(level == 1)
        def _():
            attend_own()

        @pl.when(level > 1)
        def _():
            attend_level(level - 1)

        return carry

    def attend_level(level):
        attend((z + RING - 2 * level + 1) % RING)
        attend((z + 2 * level - 1) % RING)
        attend((z + RING - 2 * level) % RING)
        attend((z + 2 * level) % RING)

    lax.fori_loop(1, 4, level_step, 0)
    z_last = (z + 8) % RING
    last_left = (z + RING - 7) % RING
    last_right = (z + 7) % RING
    for sub in range(SUBS):
        arrive(last_left, sub, 3, r2_near_right)
        arrive(last_right, sub, 3, r2_near_left)
    to_sibling(last_left).start()
    to_sibling(last_right).start()
    for sub in range(SUBS):
        arrive(z_last, sub, 3, r2_far_right if sub < SUBS // 2 else r2_far_left)
    to_sibling(z_last).start()
    attend_level(3)
    attend(last_left)
    attend(last_right)
    attend(z_last)

    osend[...] = (acc[...] / total[...]).astype(BF16)

    att_rows = pl.ds(pl.multiple_of(half * MOST, MOST), MOST)
    att_cols = pl.ds(pl.multiple_of((y * 4 + x) * HD, HD), HD)

    def back(chip_to, y_to):
        return pltpu.make_async_remote_copy(
            src_ref=osend.at[pl.ds(pl.multiple_of(chip_to * MOST, MOST), MOST), :],
            dst_ref=att.at[att_rows, att_cols],
            send_sem=s3, recv_sem=r3,
            device_id=(ctx_of(chip_to, core), y_to), device_id_type=MESH,
        )

    for step in range(1, 4):
        back(chip, (y + step) % 4).start()

    def backs(r, carry):
        chip_to = (chip + r) % CHIPS
        for step in range(4):
            back(chip_to, (y + step) % 4).start()
        return carry

    lax.fori_loop(1, CHIPS, backs, 0)
    att[att_rows, att_cols] = osend[my_q_rows, :]

    def pass_on(step):
        y_from = (y + 4 - step) % 4
        rows = pl.ds(pl.multiple_of(y_from * w_rows + core * half_rows, half_rows), half_rows)
        pltpu.make_async_copy(wbuf.at[rows, :], wbuf.at[rows, :], r_w.at[step - 1]).wait()
        pltpu.make_async_remote_copy(
            src_ref=wbuf.at[rows, :], dst_ref=wbuf.at[rows, :],
            send_sem=s_wf, recv_sem=r_wf,
            device_id=(sibling, y), device_id_type=MESH,
        ).start()

    for step in (1, 3, 2):
        pass_on(step)
    own_w.wait()
    three = wbuf.at[pl.ds(0, 3 * half_rows), :]
    pltpu.make_async_copy(three, three, r_wf).wait()
    pltpu.make_async_copy(kv.at[pl.ds(0, 31 * MOST), :], kv.at[pl.ds(0, 31 * MOST), :], r3).wait()

    updates = jnp.dot(att[...], wbuf[...], preferred_element_type=F32) * rsel[...]
    updates = updates.astype(BF16)
    for hf in range(2):
        out_ref[hf * PIECE : (hf + 1) * PIECE, :] = jnp.dot(
            place[hf], updates[hf * MOST : (hf + 1) * MOST, :], preferred_element_type=F32
        ).astype(BF16)

    pltpu.make_async_copy(arrived, arrived, s1).wait()
    pltpu.make_async_copy(pad_other, pad_other, s1).wait()
    sent = kv.at[pl.ds(0, 15 * PICK), :]
    pltpu.make_async_copy(sent, sent, s2).wait()
    sent = kv.at[pl.ds(0, 16 * PICK), :]
    pltpu.make_async_copy(sent, sent, s_sib).wait()
    sent = kv.at[pl.ds(0, 31 * MOST), :]
    pltpu.make_async_copy(sent, sent, s3).wait()
    pltpu.make_async_copy(three, three, s_w).wait()
    pltpu.make_async_copy(three, three, s_wf).wait()


def shards(queries, key_proj, value_proj, router, chosen, out_weight):
    tok_rows = queries.shape[0]
    w_cols = out_weight.shape[1] // 4
    dma = pltpu.SemaphoreType.DMA
    vmem = pl.BlockSpec(memory_space=pltpu.VMEM)
    hbm = pl.BlockSpec(memory_space=pltpu.HBM)
    return pl.pallas_call(
        body,
        out_shape=jax.ShapeDtypeStruct((tok_rows, w_cols), BF16),
        in_specs=[hbm] * 3 + [vmem] + [hbm] * 2,
        out_specs=vmem,
        scratch_shapes=[
            pltpu.VMEM(queries.shape, BF16),
            pltpu.VMEM(key_proj.shape, BF16),
            pltpu.VMEM(value_proj.shape, BF16),
            pltpu.VMEM(chosen.shape, jnp.int32),
            dma((4,)),
            pltpu.VMEM((CHIPS, 3, MOST, HD), BF16),
            pltpu.VMEM((CHIPS, 2, MOST, HD), BF16),
            pltpu.VMEM((CHIPS, MOST, HD), BF16),
            pltpu.VMEM((2 * RING * PICK, HD), BF16),
            pltpu.VMEM((2 * MOST, 16 * HD), BF16),
            pltpu.VMEM((CHIPS * MOST, HD), BF16),
            pltpu.VMEM((4 * out_weight.shape[0], w_cols), BF16),
            pltpu.VMEM((2, PIECE, MOST), BF16),
            pltpu.VMEM((2 * MOST, 1), F32),
            pltpu.VMEM((CHIPS * MOST, 1), F32),
            pltpu.VMEM((CHIPS * MOST, 1), F32),
            pltpu.VMEM((CHIPS * MOST, HD), F32),
            pltpu.VMEM((PICK, GROUP * MOST), BF16),
            dma, dma, dma,
            dma, *[dma((4 * SUBS,))] * 4,
            dma, dma((RING,)),
            dma, dma,
            dma, dma((3,)), dma, dma, dma,
        ],
        compiler_params=pltpu.CompilerParams(
            collective_id=0, has_side_effects=True, vmem_limit_bytes=60 * 1024 * 1024
        ),
        name="routed_attention",
    )(queries, key_proj, value_proj, router.reshape(1, tok_rows), chosen, out_weight)


def solution(mesh):
    placed = (P("ctx", "tp"), P("ctx", "tp"), P("ctx", "tp"), P("ctx"), P(), P("tp", None))
    return jax.shard_map(
        shards, mesh=mesh, in_specs=placed, out_specs=P("ctx", "tp"), check_vma=False
    )
```

```python
import functools
import jax
import jax.numpy as jnp
from jax import lax
from jax.experimental import pallas as pl
from jax.experimental.pallas import tpu as pltpu
from jax.sharding import PartitionSpec as P

HD = 128
PIECE = 128
MOST = 32
PICK = 256
GROUP = 16
CHIPS = 8
RING = 16
SUBS = 2
SUB = PICK // SUBS
EARLY = {1: 0, 3: 1, 2: 1, 5: 3, 4: 3, 7: 5, 6: 5, 8: 7}
LATE = {2: 0, 4: 2, 6: 4, 8: 6}
ORDER = (-1, -2, "own", -3, -4, 1, 2, -5, -6, 3, 4, -7, -8, 5, 6, 7, 8)
MESH = pl.DeviceIdType.MESH
F32 = jnp.float32
BF16 = jnp.bfloat16


def z_partners():
    found = (set(), set())
    for source, stops in ((0, EARLY), (1, LATE)):
        for stop, before in stops.items():
            for way in (1, -1):
                found[(source + before) % 2].add(way * (stop - before))
                found[(source + stop) % 2].add(way * (before - stop))
    return found


def one_hots(chosen_row, base):
    first = jnp.sum((chosen_row < base).astype(jnp.int32), axis=1, keepdims=True)
    inside = (chosen_row >= base) & (chosen_row < base + PIECE)
    entry = lax.broadcasted_iota(jnp.int32, (MOST, PICK), 1)
    rank = lax.broadcasted_iota(jnp.int32, (MOST, PICK), 0)
    by_rank = (entry - first == rank) & inside
    token = lax.broadcasted_iota(jnp.int32, (PIECE, PICK), 0)
    by_token = chosen_row - base == token
    return by_rank.astype(F32).astype(BF16), by_token.astype(F32).astype(BF16)


def dot_nt(a, b):
    return lax.dot_general(a, b, (((1,), (1,)), ((), ())), preferred_element_type=F32)


def body(
    q_hbm, k_hbm, v_hbm, router_hbm, chosen_hbm, w_hbm, out_ref,
    q_ref, k_ref, v_ref, router_ref, chosen_ref, l_in, sel, pad_own, pad_other, kv, att, osend, wbuf, place, rsel, top, total, acc, pick,
    s1, r1_own, r1_other, s2, r2, s_sib, r_sib, s3, r3, s_w, r_w, s_wf, r_wf, l_w,
):
    ctx = lax.axis_index("ctx")
    y = lax.axis_index("tp")
    z = ctx // 8
    core = ctx % 2
    x = (ctx // 2) % 4
    group = ctx // GROUP
    chip = (ctx // 2) % CHIPS
    half = z % 2

    def ctx_of(chip_to, core_to):
        return group * GROUP + chip_to * 2 + core_to

    def ctx_at(z_to, core_to):
        return z_to * 8 + x * 2 + core_to

    sibling = ctx_of(chip, 1 - core)

    def at(delta):
        return (z + RING + delta) % RING

    def block_at(z_of):
        return z_of % 2 * (15 - z_of // 2 * 2) + z_of // 2

    def needs(z_to, z_from):
        return block_at(z_from) < block_at(z_to)

    block = block_at(z)
    loads = [
        pltpu.make_async_copy(src, dst, l_in.at[n])
        for n, (src, dst) in enumerate(
            ((chosen_hbm, chosen_ref), (k_hbm, k_ref), (v_hbm, v_ref), (q_hbm, q_ref), (router_hbm, router_ref))
        )
    ]
    for load in loads:
        load.start()

    barrier = pltpu.get_barrier_semaphore()

    def greet(ctx_to, y_to):
        pl.semaphore_signal(barrier, inc=1, device_id=(ctx_to, y_to), device_id_type=MESH)

    def greet_chip(r, carry):
        chip_to = (chip + r) % CHIPS
        greet(ctx_of(chip_to, core), y)
        greet(ctx_of(chip_to, 1 - core), y)
        return carry

    lax.fori_loop(1, CHIPS, greet_chip, 0)
    greet(sibling, y)
    for step in range(1, 4):
        greet(ctx, (y + step) % 4)
    even_far, odd_far = z_partners()
    even_far -= {1}
    odd_far -= {-1}
    for delta in sorted(even_far & odd_far):
        greet(ctx_at(at(delta), core), y)

    @pl.when(half == 0)
    def _():
        for delta in sorted(even_far - odd_far):
            greet(ctx_at(at(delta), core), y)

    @pl.when(half == 1)
    def _():
        for delta in sorted(odd_far - even_far):
            greet(ctx_at(at(delta), core), y)

    w_rows = w_hbm.shape[0]
    w_cols = wbuf.shape[1]
    half_rows = w_rows // 2
    own_w = pltpu.make_async_copy(
        w_hbm.at[:, pl.ds(pl.multiple_of(y * w_cols, w_cols), w_cols)],
        wbuf.at[pl.ds(pl.multiple_of(y * w_rows, w_rows), w_rows), :],
        l_w,
    )
    own_w.start()

    for load in loads:
        load.wait()

    for hf in range(2):
        piece = ctx if hf == 0 else 255 - ctx
        row = chosen_ref[pl.ds(piece // GROUP, 1), :]
        by_rank, by_token = one_hots(row, piece * PIECE)
        picks = dot_nt(by_rank, by_token)
        pick_bf = picks.astype(BF16)
        place[hf] = dot_nt(by_token, by_rank).astype(BF16)
        rows = slice(hf * PIECE, (hf + 1) * PIECE)
        rsel[hf * MOST : (hf + 1) * MOST, :] = jnp.sum(
            picks * router_ref[rows].astype(F32).reshape(1, PIECE), axis=1, keepdims=True
        )
        for kind, ref in ((1 - core, k_ref), (core, v_ref), (2, q_ref)):
            picked = jnp.dot(pick_bf, ref[rows, :], preferred_element_type=F32).astype(BF16)
            for head in range(4):
                sel[hf * 4 + head, kind] = picked[:, head * HD : (head + 1) * HD]

    pl.semaphore_wait(barrier, 18 + len(even_far) + (len(odd_far) - len(even_far)) * half)

    my_q_rows = pl.ds(pl.multiple_of(chip * MOST, MOST), MOST)

    def first_own(chip_to):
        return pltpu.make_async_remote_copy(
            src_ref=sel.at[chip_to, pl.ds(1, 2)],
            dst_ref=pad_own.at[chip],
            send_sem=s1, recv_sem=r1_own,
            device_id=(ctx_of(chip_to, core), y), device_id_type=MESH,
        )

    def first_other(chip_to):
        return pltpu.make_async_remote_copy(
            src_ref=sel.at[chip_to, 0],
            dst_ref=pad_other.at[chip],
            send_sem=s1, recv_sem=r1_other,
            device_id=(ctx_of(chip_to, 1 - core), y), device_id_type=MESH,
        )

    trips = [(dz, dx) for dz in range(2) for dx in range(4)][1:]
    for dz, dx in sorted(trips, key=lambda t: -(t[0] + min(t[1], 4 - t[1]))):
        chip_to = (half + dz) % 2 * 4 + (x + dx) % 4
        first_own(chip_to).start()
        first_other(chip_to).start()
    first_other(chip).start()
    pad_own[chip] = sel[chip, 1:3]

    def weights(step):
        y_to = (y + step) % 4
        return pltpu.make_async_remote_copy(
            src_ref=w_hbm.at[
                pl.ds(pl.multiple_of(core * half_rows, half_rows), half_rows),
                pl.ds(pl.multiple_of(y_to * w_cols, w_cols), w_cols),
            ],
            dst_ref=wbuf.at[
                pl.ds(pl.multiple_of(y * w_rows + core * half_rows, half_rows), half_rows), :
            ],
            send_sem=s_w, recv_sem=r_w.at[step - 1],
            device_id=(ctx, y_to), device_id_type=MESH,
        )

    for step in (1, 3, 2):
        weights(step).start()

    row = chosen_ref[pl.ds(block, 1), :]
    diagonal = lax.broadcasted_iota(jnp.int32, (PICK, PICK), 0) == lax.broadcasted_iota(
        jnp.int32, (PICK, PICK), 1
    )
    column = jnp.sum(jnp.where(diagonal, row, 0), axis=1, keepdims=True)

    def base_of(device):
        return block * 2048 + (half * 15 + (1 - 2 * half) * device) * PIECE

    slot = lax.broadcasted_iota(jnp.int32, (1, GROUP * MOST), 1)
    slot_core = (core + slot // (CHIPS * MOST)) % 2
    base = base_of(slot // MOST % CHIPS * 2 + slot_core)
    first = jnp.sum((column < base).astype(jnp.int32), axis=0, keepdims=True)
    inside = (column >= base) & (column < base + PIECE)
    entry = lax.broadcasted_iota(jnp.int32, (PICK, GROUP * MOST), 0)
    pick[...] = ((entry - first == slot % MOST) & inside).astype(F32).astype(BF16)
    q_place = (first + slot % MOST)[:, : CHIPS * MOST]

    arrived = pad_own.at[pl.ds(0, CHIPS - 1)]
    pltpu.make_async_copy(arrived, arrived, r1_own).wait()
    pltpu.make_async_copy(pad_other, pad_other, r1_other).wait()

    def rows_of(kind, z_from):
        return pl.ds(pl.multiple_of((kind * RING + z_from) * PICK, PICK), PICK)

    own_side = jnp.dot(
        pick[:, : CHIPS * MOST],
        pad_own[:, 0].reshape(CHIPS * MOST, HD),
        preferred_element_type=F32,
    )
    other_side = jnp.dot(
        pick[:, CHIPS * MOST :],
        pad_other[...].reshape(CHIPS * MOST, HD),
        preferred_element_type=F32,
    )
    block_rows = own_side + other_side
    top_rows, low_rows = block_rows[:HD], block_rows[HD:]

    @pl.when(core == 0)
    def _():
        kv[rows_of(core, z), :] = block_rows.astype(BF16)

    @pl.when(core == 1)
    def _():
        kv[rows_of(core, z), :] = jnp.concatenate([top_rows.T, low_rows.T], axis=0).astype(BF16)


    ways = ((0, 1), (1, -1))
    sent_rows = []

    def rows_of_sub(z_from, sub):
        return pl.ds(pl.multiple_of((core * RING + z_from) * PICK + sub * SUB, SUB), SUB)

    def arrival(side, offset, sub):
        return r2.at[(side * 8 + offset - 1) * SUBS + sub]

    def send(pred, z_from, sub, delta, side, offset):
        rows = rows_of_sub(z_from, sub)
        copy = pltpu.make_async_remote_copy(
            src_ref=kv.at[rows, :], dst_ref=kv.at[rows, :],
            send_sem=s2.at[len(sent_rows)], recv_sem=arrival(side, offset, sub),
            device_id=(ctx_at(at(delta), core), y), device_id_type=MESH,
        )
        sent_rows.append((pred, copy))

        @pl.when(pred)
        def _():
            copy.start()

    def comes(stops, z_from, side, offset, sub):
        if offset == 8 and side != sub * 2 // SUBS:
            return False
        is_wanted = needs((z_from + RING + ways[side][1] * offset) % RING, z_from)
        for stop, before in stops.items():
            if before == offset:
                further = comes(stops, z_from, side, stop, sub)
                if further is not False:
                    is_wanted = is_wanted | further
        return is_wanted

    def send_on(is_mine, stops, z_from, offset, side, sub):
        for stop, before in stops.items():
            if before == offset:
                goes = comes(stops, z_from, side, stop, sub)
                if goes is not False:
                    send(is_mine & goes, z_from, sub, ways[side][1] * (stop - offset), side, stop)

    def receive(offset):
        cases = [(half == 1, EARLY)] if offset % 2 else [(half == 0, EARLY), (half == 1, LATE)]
        for sub in range(SUBS):
            for side, way in ways:
                z_from = at(-way * offset)
                came = False
                for is_mine, stops in cases:
                    here = comes(stops, z_from, side, offset, sub)
                    if here is not False:
                        came = (is_mine & here) if came is False else came | (is_mine & here)
                if came is False:
                    continue

                @pl.when(came)
                def _():
                    rows = rows_of_sub(z_from, sub)
                    pltpu.make_async_copy(
                        kv.at[rows, :], kv.at[rows, :], arrival(side, offset, sub)
                    ).wait()

                for is_mine, stops in cases:
                    send_on(is_mine, stops, z_from, offset, side, sub)
        for z_from in (at(-offset), at(offset))[: 1 if offset == 8 else 2]:

            @pl.when(needs(z, z_from))
            def _():
                to_sibling(z_from).start()

    def to_sibling(z_from):
        rows = rows_of(core, z_from)
        return pltpu.make_async_remote_copy(
            src_ref=kv.at[rows, :], dst_ref=kv.at[rows, :],
            send_sem=s_sib.at[z_from], recv_sem=r_sib.at[z_from],
            device_id=(sibling, y), device_id_type=MESH,
        )

    for sub in range(SUBS):
        for side, way in ways:
            send_on(half == 0, EARLY, z, 0, side, sub)
            send_on(half == 1, LATE, z, 0, side, sub)
    to_sibling(z).start()

    scale = HD**-0.5 * 1.4426950408889634

    def from_sibling(z_from):
        rows = rows_of(1 - core, z_from)
        pltpu.make_async_copy(kv.at[rows, :], kv.at[rows, :], r_sib.at[z_from]).wait()

    queries = pad_own.at[:, 1]

    def scores_of(z_from):
        return dot_nt(kv[rows_of(0, z_from), :], queries[...].reshape(CHIPS * MOST, HD)) * scale

    def summed(weight, z_from):
        values = kv[rows_of(1, z_from), :]
        weight = weight.astype(BF16)
        return jnp.dot(values[:HD], weight[:HD], preferred_element_type=F32) + jnp.dot(
            values[HD:], weight[HD:], preferred_element_type=F32
        )

    def attend_own():
        from_sibling(z)
        seen = lax.broadcasted_iota(jnp.int32, (PICK, PICK), 0) <= q_place
        scores = jnp.where(seen, scores_of(z), -1e30)
        top_now = jnp.max(scores, axis=0, keepdims=True)
        weight = jnp.exp2(scores - top_now)
        top[...] = top_now
        total[...] = jnp.sum(weight, axis=0, keepdims=True)
        acc[...] = summed(weight, z)

    def attend_these(z_froms):
        scores = [scores_of(z_from) for z_from in z_froms]
        top_was = top[...]
        top_now = top_was
        for part in scores:
            top_now = jnp.maximum(top_now, jnp.max(part, axis=0, keepdims=True))
        fade = jnp.exp2(top_was - top_now)
        total_now = total[...] * fade
        acc_now = acc[...] * fade
        for part, z_from in zip(scores, z_froms):
            weight = jnp.exp2(part - top_now)
            total_now += jnp.sum(weight, axis=0, keepdims=True)
            acc_now += summed(weight, z_from)
        top[...] = top_now
        total[...] = total_now
        acc[...] = acc_now

    def attend(z_from):
        @pl.when(needs(z, z_from))
        def _():
            from_sibling(z_from)
            attend_these([z_from])

    def attend_both(offset):
        left, right = at(-offset), at(offset)
        wants_left, wants_right = needs(z, left), needs(z, right)

        @pl.when(wants_left)
        def _():
            from_sibling(left)

        @pl.when(wants_right)
        def _():
            from_sibling(right)

        @pl.when(wants_left & wants_right)
        def _():
            attend_these([left, right])

        @pl.when(wants_left != wants_right)
        def _():
            attend_these([lax.select(wants_left, left, right)])

    for step in ORDER:
        if step == "own":
            attend_own()
        elif step < 0:
            receive(-step)
        elif step == 8:
            attend(at(8))
        else:
            attend_both(step)

    osend[...] = (acc[...] / total[...]).T.astype(BF16)

    att_rows = pl.ds(pl.multiple_of(half * MOST, MOST), MOST)
    att_cols = pl.ds(pl.multiple_of((y * 4 + x) * HD, HD), HD)

    def back(chip_to, y_to):
        return pltpu.make_async_remote_copy(
            src_ref=osend.at[pl.ds(pl.multiple_of(chip_to * MOST, MOST), MOST), :],
            dst_ref=att.at[att_rows, att_cols],
            send_sem=s3, recv_sem=r3,
            device_id=(ctx_of(chip_to, core), y_to), device_id_type=MESH,
        )

    def steps(there):
        return min(there, 4 - there)

    trips = [(dz, dx, dy) for dz in range(2) for dx in range(4) for dy in range(4)][1:]
    for dz, dx, dy in sorted(trips, key=lambda t: -(t[0] + steps(t[1]) + steps(t[2]))):
        back((half + dz) % 2 * 4 + (x + dx) % 4, (y + dy) % 4).start()
    att[att_rows, att_cols] = osend[my_q_rows, :]

    def pass_on(step):
        y_from = (y + 4 - step) % 4
        rows = pl.ds(pl.multiple_of(y_from * w_rows + core * half_rows, half_rows), half_rows)
        pltpu.make_async_copy(wbuf.at[rows, :], wbuf.at[rows, :], r_w.at[step - 1]).wait()
        pltpu.make_async_remote_copy(
            src_ref=wbuf.at[rows, :], dst_ref=wbuf.at[rows, :],
            send_sem=s_wf, recv_sem=r_wf,
            device_id=(sibling, y), device_id_type=MESH,
        ).start()

    for step in (1, 3, 2):
        pass_on(step)
    own_w.wait()
    three = wbuf.at[pl.ds(0, 3 * half_rows), :]
    pltpu.make_async_copy(three, three, r_wf).wait()
    pltpu.make_async_copy(kv.at[pl.ds(0, 31 * MOST), :], kv.at[pl.ds(0, 31 * MOST), :], r3).wait()

    updates = jnp.dot(att[...], wbuf[...], preferred_element_type=F32) * rsel[...]
    updates = updates.astype(BF16)
    for hf in range(2):
        out_ref[hf * PIECE : (hf + 1) * PIECE, :] = jnp.dot(
            place[hf], updates[hf * MOST : (hf + 1) * MOST, :], preferred_element_type=F32
        ).astype(BF16)

    pltpu.make_async_copy(arrived, arrived, s1).wait()
    pltpu.make_async_copy(pad_other, pad_other, s1).wait()
    for pred, copy in sent_rows:

        @pl.when(pred)
        def _():
            copy.wait_send()

    def sibling_sent(z_from, carry):
        @pl.when(needs(z, z_from) | (z_from == z))
        def _():
            to_sibling(z_from).wait_send()

        return carry

    lax.fori_loop(0, RING, sibling_sent, 0)
    sent = kv.at[pl.ds(0, 31 * MOST), :]
    pltpu.make_async_copy(sent, sent, s3).wait()
    pltpu.make_async_copy(three, three, s_w).wait()
    pltpu.make_async_copy(three, three, s_wf).wait()


def shards(queries, key_proj, value_proj, router, chosen, out_weight):
    tok_rows = queries.shape[0]
    w_cols = out_weight.shape[1] // 4
    dma = pltpu.SemaphoreType.DMA
    vmem = pl.BlockSpec(memory_space=pltpu.VMEM)
    hbm = pl.BlockSpec(memory_space=pltpu.HBM)
    return pl.pallas_call(
        body,
        out_shape=jax.ShapeDtypeStruct((tok_rows, w_cols), BF16),
        in_specs=[hbm] * 6,
        out_specs=vmem,
        scratch_shapes=[
            pltpu.VMEM(queries.shape, BF16),
            pltpu.VMEM(key_proj.shape, BF16),
            pltpu.VMEM(value_proj.shape, BF16),
            pltpu.VMEM(router.shape, BF16),
            pltpu.VMEM(chosen.shape, jnp.int32),
            dma((5,)),
            pltpu.VMEM((CHIPS, 3, MOST, HD), BF16),
            pltpu.VMEM((CHIPS, 2, MOST, HD), BF16),
            pltpu.VMEM((CHIPS, MOST, HD), BF16),
            pltpu.VMEM((2 * RING * PICK, HD), BF16),
            pltpu.VMEM((2 * MOST, 16 * HD), BF16),
            pltpu.VMEM((CHIPS * MOST, HD), BF16),
            pltpu.VMEM((4 * out_weight.shape[0], w_cols), BF16),
            pltpu.VMEM((2, PIECE, MOST), BF16),
            pltpu.VMEM((2 * MOST, 1), F32),
            pltpu.VMEM((1, CHIPS * MOST), F32),
            pltpu.VMEM((1, CHIPS * MOST), F32),
            pltpu.VMEM((HD, CHIPS * MOST), F32),
            pltpu.VMEM((PICK, GROUP * MOST), BF16),
            dma, dma, dma,
            dma((64,)), dma((16 * SUBS,)),
            dma((RING,)), dma((RING,)),
            dma, dma,
            dma, dma((3,)), dma, dma, dma,
        ],
        compiler_params=pltpu.CompilerParams(
            collective_id=0, has_side_effects=True, vmem_limit_bytes=60 * 1024 * 1024
        ),
        name="routed_attention",
    )(queries, key_proj, value_proj, router, chosen, out_weight)


def solution(mesh):
    placed = (P("ctx", "tp"), P("ctx", "tp"), P("ctx", "tp"), P("ctx"), P(), P("tp", None))
    return jax.shard_map(
        shards, mesh=mesh, in_specs=placed, out_specs=P("ctx", "tp"), check_vma=False
    )
```

```python
import functools
import jax
import jax.numpy as jnp
from jax import lax
from jax.experimental import pallas as pl
from jax.experimental.pallas import tpu as pltpu
from jax.sharding import PartitionSpec as P

HD = 128
PIECE = 128
MOST = 32
PICK = 256
GROUP = 16
CHIPS = 8
RING = 16
SUBS = 2
SUB = PICK // SUBS
EARLY = {1: 0, 3: 1, 2: 1, 5: 3, 4: 3, 7: 5, 6: 5, 8: 7}
LATE = {2: 0, 4: 2, 6: 4, 8: 6}
ORDER = (-1, -2, "own", -3, -4, 1, 2, -5, -6, "share", 3, 4, -7, -8, 5, 6, 7, 8)
MESH = pl.DeviceIdType.MESH
F32 = jnp.float32
BF16 = jnp.bfloat16


def z_partners():
    found = (set(), set())
    for source, stops in ((0, EARLY), (1, LATE)):
        for stop, before in stops.items():
            for way in (1, -1):
                found[(source + before) % 2].add(way * (stop - before))
                found[(source + stop) % 2].add(way * (before - stop))
    return found


def one_hots(chosen_row, base):
    first = jnp.sum((chosen_row < base).astype(jnp.int32), axis=1, keepdims=True)
    inside = (chosen_row >= base) & (chosen_row < base + PIECE)
    entry = lax.broadcasted_iota(jnp.int32, (MOST, PICK), 1)
    rank = lax.broadcasted_iota(jnp.int32, (MOST, PICK), 0)
    by_rank = (entry - first == rank) & inside
    token = lax.broadcasted_iota(jnp.int32, (PIECE, PICK), 0)
    by_token = chosen_row - base == token
    return by_rank.astype(F32).astype(BF16), by_token.astype(F32).astype(BF16)


def dot_nt(a, b):
    return lax.dot_general(a, b, (((1,), (1,)), ((), ())), preferred_element_type=F32)


def body(
    q_hbm, k_hbm, v_hbm, router_hbm, chosen_hbm, w_hbm, out_ref,
    q_ref, k_ref, v_ref, router_ref, chosen_ref, l_in, sel, pad_own, pad_other, pad_query, kv, att, osend, wbuf, place, rsel, top, total, acc, pick,
    s1, r1_own, r1_other, r1_query, s2, r2, s_sib, r_sib, s3, r3, s_w, r_w, s_wf, r_wf, l_w,
):
    ctx = lax.axis_index("ctx")
    y = lax.axis_index("tp")
    z = ctx // 8
    core = ctx % 2
    x = (ctx // 2) % 4
    group = ctx // GROUP
    chip = (ctx // 2) % CHIPS
    half = z % 2

    def ctx_of(chip_to, core_to):
        return group * GROUP + chip_to * 2 + core_to

    def ctx_at(z_to, core_to):
        return z_to * 8 + x * 2 + core_to

    sibling = ctx_of(chip, 1 - core)

    def at(delta):
        return (z + RING + delta) % RING

    def block_at(z_of):
        return z_of % 2 * (15 - z_of // 2 * 2) + z_of // 2

    def needs(z_to, z_from):
        return block_at(z_from) < block_at(z_to)

    block = block_at(z)
    loads = [
        pltpu.make_async_copy(src, dst, l_in.at[n])
        for n, (src, dst) in enumerate(
            ((chosen_hbm, chosen_ref), (k_hbm, k_ref), (v_hbm, v_ref), (q_hbm, q_ref), (router_hbm, router_ref))
        )
    ]
    for load in loads:
        load.start()

    barrier = pltpu.get_barrier_semaphore()

    def greet(ctx_to, y_to):
        pl.semaphore_signal(barrier, inc=1, device_id=(ctx_to, y_to), device_id_type=MESH)

    def greet_chip(r, carry):
        chip_to = (chip + r) % CHIPS
        greet(ctx_of(chip_to, core), y)
        greet(ctx_of(chip_to, 1 - core), y)
        return carry

    lax.fori_loop(1, CHIPS, greet_chip, 0)
    greet(sibling, y)
    for step in range(1, 4):
        greet(ctx, (y + step) % 4)
    even_far, odd_far = z_partners()
    even_far -= {1}
    odd_far -= {-1}
    for delta in sorted(even_far & odd_far):
        greet(ctx_at(at(delta), core), y)

    @pl.when(half == 0)
    def _():
        for delta in sorted(even_far - odd_far):
            greet(ctx_at(at(delta), core), y)

    @pl.when(half == 1)
    def _():
        for delta in sorted(odd_far - even_far):
            greet(ctx_at(at(delta), core), y)

    w_rows = w_hbm.shape[0]
    w_cols = wbuf.shape[1]
    half_rows = w_rows // 2
    own_w = pltpu.make_async_copy(
        w_hbm.at[:, pl.ds(pl.multiple_of(y * w_cols, w_cols), w_cols)],
        wbuf.at[pl.ds(pl.multiple_of(y * w_rows, w_rows), w_rows), :],
        l_w,
    )
    own_w.start()

    for load in loads[:3]:
        load.wait()

    picks_of = []
    ones = []

    def select(hf, kind, ref):
        picked = jnp.dot(
            picks_of[hf], ref[hf * PIECE : (hf + 1) * PIECE, :], preferred_element_type=F32
        ).astype(BF16)
        for head in range(4):
            sel[hf * 4 + head, kind] = picked[:, head * HD : (head + 1) * HD]

    for hf in range(2):
        piece = ctx if hf == 0 else 255 - ctx
        row = chosen_ref[pl.ds(piece // GROUP, 1), :]
        by_rank, by_token = one_hots(row, piece * PIECE)
        picks = dot_nt(by_rank, by_token)
        ones.append((by_rank, by_token, picks))
        picks_of.append(picks.astype(BF16))
        for kind, ref in ((1 - core, k_ref), (core, v_ref)):
            select(hf, kind, ref)

    pl.semaphore_wait(barrier, 18 + len(even_far) + (len(odd_far) - len(even_far)) * half)

    my_q_rows = pl.ds(pl.multiple_of(chip * MOST, MOST), MOST)

    def first_own(chip_to):
        return pltpu.make_async_remote_copy(
            src_ref=sel.at[chip_to, 1],
            dst_ref=pad_own.at[chip],
            send_sem=s1, recv_sem=r1_own,
            device_id=(ctx_of(chip_to, core), y), device_id_type=MESH,
        )

    def first_query(chip_to):
        return pltpu.make_async_remote_copy(
            src_ref=sel.at[chip_to, 2],
            dst_ref=pad_query.at[chip],
            send_sem=s1, recv_sem=r1_query,
            device_id=(ctx_of(chip_to, core), y), device_id_type=MESH,
        )

    def first_other(chip_to):
        return pltpu.make_async_remote_copy(
            src_ref=sel.at[chip_to, 0],
            dst_ref=pad_other.at[chip],
            send_sem=s1, recv_sem=r1_other,
            device_id=(ctx_of(chip_to, 1 - core), y), device_id_type=MESH,
        )

    trips = [(dz, dx) for dz in range(2) for dx in range(4)][1:]
    for dz, dx in sorted(trips, key=lambda t: -(t[0] + min(t[1], 4 - t[1]))):
        chip_to = (half + dz) % 2 * 4 + (x + dx) % 4
        first_own(chip_to).start()
        first_other(chip_to).start()
    first_other(chip).start()
    pad_own[chip] = sel[chip, 1]
    loads[3].wait()
    for hf in range(2):
        select(hf, 2, q_ref)
    for dz, dx in trips:
        first_query((half + dz) % 2 * 4 + (x + dx) % 4).start()
    pad_query[chip] = sel[chip, 2]
    loads[4].wait()
    for hf, (by_rank, by_token, picks) in enumerate(ones):
        place[hf] = dot_nt(by_token, by_rank).astype(BF16)
        rows = slice(hf * PIECE, (hf + 1) * PIECE)
        rsel[hf * MOST : (hf + 1) * MOST, :] = jnp.sum(
            picks * router_ref[rows].astype(F32).reshape(1, PIECE), axis=1, keepdims=True
        )

    quarter_rows = w_rows // 4
    beside = ctx + 2 - x % 2 * 4

    def weight_rows(y_from, step, x_of):
        if step == 2:
            first_row = y_from * w_rows + (x_of % 2 * 2 + core) * quarter_rows
            return pl.ds(pl.multiple_of(first_row, quarter_rows), quarter_rows)
        return pl.ds(pl.multiple_of(y_from * w_rows + core * half_rows, half_rows), half_rows)

    def weights(step):
        y_to = (y + step) % 4
        return pltpu.make_async_remote_copy(
            src_ref=w_hbm.at[
                weight_rows(0, step, x), pl.ds(pl.multiple_of(y_to * w_cols, w_cols), w_cols)
            ],
            dst_ref=wbuf.at[weight_rows(y, step, x), :],
            send_sem=s_w, recv_sem=r_w.at[step - 1],
            device_id=(ctx, y_to), device_id_type=MESH,
        )

    def pass_on(rows, arrived_by, to, lands_by):
        pltpu.make_async_copy(wbuf.at[rows, :], wbuf.at[rows, :], arrived_by).wait()
        for ctx_to, sem in zip(to, lands_by):
            pltpu.make_async_remote_copy(
                src_ref=wbuf.at[rows, :], dst_ref=wbuf.at[rows, :],
                send_sem=s_wf, recv_sem=sem,
                device_id=(ctx_to, y), device_id_type=MESH,
            ).start()

    def share_weights():
        rows = weight_rows((y + 2) % 4, 2, x)
        pass_on(rows, r_w.at[1], (beside, sibling), (r_w.at[3], r_wf))

    def finish_weights():
        pass_on(weight_rows((y + 3) % 4, 1, x), r_w.at[0], (sibling,), (r_wf,))
        pass_on(weight_rows((y + 1) % 4, 3, x), r_w.at[2], (sibling,), (r_wf,))
        pass_on(weight_rows((y + 2) % 4, 2, x + 1), r_w.at[3], (sibling,), (r_wf,))

    for step in (2, 1, 3):
        weights(step).start()

    row = chosen_ref[pl.ds(block, 1), :]
    diagonal = lax.broadcasted_iota(jnp.int32, (PICK, PICK), 0) == lax.broadcasted_iota(
        jnp.int32, (PICK, PICK), 1
    )
    column = jnp.sum(jnp.where(diagonal, row, 0), axis=1, keepdims=True)

    def base_of(device):
        return block * 2048 + (half * 15 + (1 - 2 * half) * device) * PIECE

    slot = lax.broadcasted_iota(jnp.int32, (1, GROUP * MOST), 1)
    slot_core = (core + slot // (CHIPS * MOST)) % 2
    base = base_of(slot // MOST % CHIPS * 2 + slot_core)
    first = jnp.sum((column < base).astype(jnp.int32), axis=0, keepdims=True)
    inside = (column >= base) & (column < base + PIECE)
    entry = lax.broadcasted_iota(jnp.int32, (PICK, GROUP * MOST), 0)
    pick[...] = ((entry - first == slot % MOST) & inside).astype(F32).astype(BF16)
    q_place = (first + slot % MOST)[:, : CHIPS * MOST]

    arrived = pad_own.at[pl.ds(0, CHIPS - 1)]
    pltpu.make_async_copy(arrived, arrived, r1_own).wait()
    pltpu.make_async_copy(pad_other, pad_other, r1_other).wait()

    def rows_of(kind, z_from):
        return pl.ds(pl.multiple_of((kind * RING + z_from) * PICK, PICK), PICK)

    own_side = jnp.dot(
        pick[:, : CHIPS * MOST],
        pad_own[...].reshape(CHIPS * MOST, HD),
        preferred_element_type=F32,
    )
    other_side = jnp.dot(
        pick[:, CHIPS * MOST :],
        pad_other[...].reshape(CHIPS * MOST, HD),
        preferred_element_type=F32,
    )
    block_rows = own_side + other_side
    top_rows, low_rows = block_rows[:HD], block_rows[HD:]

    @pl.when(core == 0)
    def _():
        kv[rows_of(core, z), :] = block_rows.astype(BF16)

    @pl.when(core == 1)
    def _():
        kv[rows_of(core, z), :] = jnp.concatenate([top_rows.T, low_rows.T], axis=0).astype(BF16)


    ways = ((0, 1), (1, -1))
    sent_rows = []

    def rows_of_sub(z_from, sub):
        return pl.ds(pl.multiple_of((core * RING + z_from) * PICK + sub * SUB, SUB), SUB)

    def arrival(side, offset, sub):
        return r2.at[(side * 8 + offset - 1) * SUBS + sub]

    def send(pred, z_from, sub, delta, side, offset):
        rows = rows_of_sub(z_from, sub)
        copy = pltpu.make_async_remote_copy(
            src_ref=kv.at[rows, :], dst_ref=kv.at[rows, :],
            send_sem=s2.at[len(sent_rows)], recv_sem=arrival(side, offset, sub),
            device_id=(ctx_at(at(delta), core), y), device_id_type=MESH,
        )
        sent_rows.append((pred, copy))

        @pl.when(pred)
        def _():
            copy.start()

    def comes(stops, z_from, side, offset, sub):
        if offset == 8 and side != sub * 2 // SUBS:
            return False
        is_wanted = needs((z_from + RING + ways[side][1] * offset) % RING, z_from)
        for stop, before in stops.items():
            if before == offset:
                further = comes(stops, z_from, side, stop, sub)
                if further is not False:
                    is_wanted = is_wanted | further
        return is_wanted

    def send_on(is_mine, stops, z_from, offset, side, sub):
        for stop, before in stops.items():
            if before == offset:
                goes = comes(stops, z_from, side, stop, sub)
                if goes is not False:
                    send(is_mine & goes, z_from, sub, ways[side][1] * (stop - offset), side, stop)

    def receive(offset):
        cases = [(half == 1, EARLY)] if offset % 2 else [(half == 0, EARLY), (half == 1, LATE)]
        for sub in range(SUBS):
            for side, way in ways:
                z_from = at(-way * offset)
                came = False
                for is_mine, stops in cases:
                    here = comes(stops, z_from, side, offset, sub)
                    if here is not False:
                        came = (is_mine & here) if came is False else came | (is_mine & here)
                if came is False:
                    continue

                @pl.when(came)
                def _():
                    rows = rows_of_sub(z_from, sub)
                    pltpu.make_async_copy(
                        kv.at[rows, :], kv.at[rows, :], arrival(side, offset, sub)
                    ).wait()

                for is_mine, stops in cases:
                    send_on(is_mine, stops, z_from, offset, side, sub)
        for z_from in (at(-offset), at(offset))[: 1 if offset == 8 else 2]:

            @pl.when(needs(z, z_from))
            def _():
                to_sibling(z_from).start()

    def to_sibling(z_from):
        rows = rows_of(core, z_from)
        return pltpu.make_async_remote_copy(
            src_ref=kv.at[rows, :], dst_ref=kv.at[rows, :],
            send_sem=s_sib.at[z_from], recv_sem=r_sib.at[z_from],
            device_id=(sibling, y), device_id_type=MESH,
        )

    for sub in range(SUBS):
        for side, way in ways:
            send_on(half == 0, EARLY, z, 0, side, sub)
            send_on(half == 1, LATE, z, 0, side, sub)
    to_sibling(z).start()

    pltpu.make_async_copy(arrived, arrived, r1_query).wait()

    scale = HD**-0.5 * 1.4426950408889634

    def from_sibling(z_from):
        rows = rows_of(1 - core, z_from)
        pltpu.make_async_copy(kv.at[rows, :], kv.at[rows, :], r_sib.at[z_from]).wait()


    def scores_of(z_from):
        return dot_nt(kv[rows_of(0, z_from), :], pad_query[...].reshape(CHIPS * MOST, HD)) * scale

    def summed(weight, z_from):
        values = kv[rows_of(1, z_from), :]
        weight = weight.astype(BF16)
        return jnp.dot(values[:HD], weight[:HD], preferred_element_type=F32) + jnp.dot(
            values[HD:], weight[HD:], preferred_element_type=F32
        )

    def attend_own():
        from_sibling(z)
        seen = lax.broadcasted_iota(jnp.int32, (PICK, PICK), 0) <= q_place
        scores = jnp.where(seen, scores_of(z), -1e30)
        top_now = jnp.max(scores, axis=0, keepdims=True)
        weight = jnp.exp2(scores - top_now)
        top[...] = top_now
        total[...] = jnp.sum(weight, axis=0, keepdims=True)
        acc[...] = summed(weight, z)

    def attend_these(z_froms):
        scores = [scores_of(z_from) for z_from in z_froms]
        top_was = top[...]
        top_now = top_was
        for part in scores:
            top_now = jnp.maximum(top_now, jnp.max(part, axis=0, keepdims=True))
        fade = jnp.exp2(top_was - top_now)
        total_now = total[...] * fade
        acc_now = acc[...] * fade
        for part, z_from in zip(scores, z_froms):
            weight = jnp.exp2(part - top_now)
            total_now += jnp.sum(weight, axis=0, keepdims=True)
            acc_now += summed(weight, z_from)
        top[...] = top_now
        total[...] = total_now
        acc[...] = acc_now

    def attend(z_from):
        @pl.when(needs(z, z_from))
        def _():
            from_sibling(z_from)
            attend_these([z_from])

    def attend_both(offset):
        left, right = at(-offset), at(offset)
        wants_left, wants_right = needs(z, left), needs(z, right)

        @pl.when(wants_left)
        def _():
            from_sibling(left)

        @pl.when(wants_right)
        def _():
            from_sibling(right)

        @pl.when(wants_left & wants_right)
        def _():
            attend_these([left, right])

        @pl.when(wants_left != wants_right)
        def _():
            attend_these([lax.select(wants_left, left, right)])

    for step in ORDER:
        if step == "own":
            attend_own()
        elif step == "share":
            share_weights()
        elif step < 0:
            receive(-step)
        elif step == 8:
            attend(at(8))
        else:
            attend_both(step)

    osend[...] = (acc[...] / total[...]).T.astype(BF16)

    att_rows = pl.ds(pl.multiple_of(half * MOST, MOST), MOST)
    att_cols = pl.ds(pl.multiple_of((y * 4 + x) * HD, HD), HD)

    def back(chip_to, y_to):
        return pltpu.make_async_remote_copy(
            src_ref=osend.at[pl.ds(pl.multiple_of(chip_to * MOST, MOST), MOST), :],
            dst_ref=att.at[att_rows, att_cols],
            send_sem=s3, recv_sem=r3,
            device_id=(ctx_of(chip_to, core), y_to), device_id_type=MESH,
        )

    def steps(there):
        return min(there, 4 - there)

    trips = [(dz, dx, dy) for dz in range(2) for dx in range(4) for dy in range(4)][1:]
    for dz, dx, dy in sorted(trips, key=lambda t: -(t[0] + steps(t[1]) + steps(t[2]))):
        back((half + dz) % 2 * 4 + (x + dx) % 4, (y + dy) % 4).start()
    att[att_rows, att_cols] = osend[my_q_rows, :]

    finish_weights()
    own_w.wait()
    three = wbuf.at[pl.ds(0, 3 * half_rows), :]
    pltpu.make_async_copy(three, three, r_wf).wait()
    pltpu.make_async_copy(kv.at[pl.ds(0, 31 * MOST), :], kv.at[pl.ds(0, 31 * MOST), :], r3).wait()

    updates = jnp.dot(att[...], wbuf[...], preferred_element_type=F32) * rsel[...]
    updates = updates.astype(BF16)
    for hf in range(2):
        out_ref[hf * PIECE : (hf + 1) * PIECE, :] = jnp.dot(
            place[hf], updates[hf * MOST : (hf + 1) * MOST, :], preferred_element_type=F32
        ).astype(BF16)

    pltpu.make_async_copy(arrived, arrived, s1).wait()
    pltpu.make_async_copy(arrived, arrived, s1).wait()
    pltpu.make_async_copy(pad_other, pad_other, s1).wait()
    for pred, copy in sent_rows:

        @pl.when(pred)
        def _():
            copy.wait_send()

    def sibling_sent(z_from, carry):
        @pl.when(needs(z, z_from) | (z_from == z))
        def _():
            to_sibling(z_from).wait_send()

        return carry

    lax.fori_loop(0, RING, sibling_sent, 0)
    sent = kv.at[pl.ds(0, 31 * MOST), :]
    pltpu.make_async_copy(sent, sent, s3).wait()
    for rows, sem in ((5 * quarter_rows, s_w), (7 * quarter_rows, s_wf)):
        sent = wbuf.at[pl.ds(0, rows), :]
        pltpu.make_async_copy(sent, sent, sem).wait()


def shards(queries, key_proj, value_proj, router, chosen, out_weight):
    tok_rows = queries.shape[0]
    w_cols = out_weight.shape[1] // 4
    dma = pltpu.SemaphoreType.DMA
    vmem = pl.BlockSpec(memory_space=pltpu.VMEM)
    hbm = pl.BlockSpec(memory_space=pltpu.HBM)
    return pl.pallas_call(
        body,
        out_shape=jax.ShapeDtypeStruct((tok_rows, w_cols), BF16),
        in_specs=[hbm] * 6,
        out_specs=vmem,
        scratch_shapes=[
            pltpu.VMEM(queries.shape, BF16),
            pltpu.VMEM(key_proj.shape, BF16),
            pltpu.VMEM(value_proj.shape, BF16),
            pltpu.VMEM(router.shape, BF16),
            pltpu.VMEM(chosen.shape, jnp.int32),
            dma((5,)),
            pltpu.VMEM((CHIPS, 3, MOST, HD), BF16),
            *[pltpu.VMEM((CHIPS, MOST, HD), BF16)] * 3,
            pltpu.VMEM((2 * RING * PICK, HD), BF16),
            pltpu.VMEM((2 * MOST, 16 * HD), BF16),
            pltpu.VMEM((CHIPS * MOST, HD), BF16),
            pltpu.VMEM((4 * out_weight.shape[0], w_cols), BF16),
            pltpu.VMEM((2, PIECE, MOST), BF16),
            pltpu.VMEM((2 * MOST, 1), F32),
            pltpu.VMEM((1, CHIPS * MOST), F32),
            pltpu.VMEM((1, CHIPS * MOST), F32),
            pltpu.VMEM((HD, CHIPS * MOST), F32),
            pltpu.VMEM((PICK, GROUP * MOST), BF16),
            dma, dma, dma, dma,
            dma((64,)), dma((16 * SUBS,)),
            dma((RING,)), dma((RING,)),
            dma, dma,
            dma, dma((4,)), dma, dma, dma,
        ],
        compiler_params=pltpu.CompilerParams(
            collective_id=0, has_side_effects=True, vmem_limit_bytes=60 * 1024 * 1024
        ),
        name="routed_attention",
    )(queries, key_proj, value_proj, router, chosen, out_weight)


def solution(mesh):
    placed = (P("ctx", "tp"), P("ctx", "tp"), P("ctx", "tp"), P("ctx"), P(), P("tp", None))
    return jax.shard_map(
        shards, mesh=mesh, in_specs=placed, out_specs=P("ctx", "tp"), check_vma=False
    )
```

```python
import functools
import jax
import jax.numpy as jnp
from jax import lax
from jax.experimental import pallas as pl
from jax.experimental.pallas import tpu as pltpu
from jax.sharding import PartitionSpec as P

HD = 128
PIECE = 128
MOST = 32
PICK = 256
GROUP = 16
CHIPS = 8
RING = 16
SUBS = 2
SUB = PICK // SUBS
EARLY = {1: 0, 3: 1, 2: 1, 5: 3, 4: 3, 7: 5, 6: 5, 8: 7}
LATE = {2: 0, 4: 2, 6: 4, 8: 6}
ORDER = (-1, -2, "own", -3, -4, 1, 2, -5, -6, "share", 3, 4, 5, 6, -7, -8, 7, 8)
MESH = pl.DeviceIdType.MESH
F32 = jnp.float32
BF16 = jnp.bfloat16


def z_partners():
    found = (set(), set())
    for source, stops in ((0, EARLY), (1, LATE)):
        for stop, before in stops.items():
            for way in (1, -1):
                found[(source + before) % 2].add(way * (stop - before))
                found[(source + stop) % 2].add(way * (before - stop))
    return found


def one_hots(chosen_row, base):
    first = jnp.sum((chosen_row < base).astype(jnp.int32), axis=1, keepdims=True)
    inside = (chosen_row >= base) & (chosen_row < base + PIECE)
    entry = lax.broadcasted_iota(jnp.int32, (MOST, PICK), 1)
    rank = lax.broadcasted_iota(jnp.int32, (MOST, PICK), 0)
    by_rank = (entry - first == rank) & inside
    token = lax.broadcasted_iota(jnp.int32, (PIECE, PICK), 0)
    by_token = chosen_row - base == token
    return by_rank.astype(F32).astype(BF16), by_token.astype(F32).astype(BF16)


def dot_nt(a, b):
    return lax.dot_general(a, b, (((1,), (1,)), ((), ())), preferred_element_type=F32)


def body(
    q_hbm, k_hbm, v_hbm, router_hbm, chosen_hbm, w_hbm, out_ref,
    q_ref, k_ref, v_ref, router_ref, chosen_ref, l_in, sel, pad_own, pad_other, pad_query, kv, att, osend, wbuf, place, rsel, top, total, acc, pick,
    s1, r1_own, r1_other, r1_query, s2, r2, s_sib, r_sib, s3, r3, s_w, r_w, s_wf, r_wf, l_w,
):
    ctx = lax.axis_index("ctx")
    y = lax.axis_index("tp")
    z = ctx // 8
    core = ctx % 2
    x = (ctx // 2) % 4
    group = ctx // GROUP
    chip = (ctx // 2) % CHIPS
    half = z % 2

    def ctx_of(chip_to, core_to):
        return group * GROUP + chip_to * 2 + core_to

    def ctx_at(z_to, core_to):
        return z_to * 8 + x * 2 + core_to

    sibling = ctx_of(chip, 1 - core)

    def at(delta):
        return (z + RING + delta) % RING

    def block_at(z_of):
        return z_of % 2 * (15 - z_of // 2 * 2) + z_of // 2

    def needs(z_to, z_from):
        return block_at(z_from) < block_at(z_to)

    block = block_at(z)
    loads = [
        pltpu.make_async_copy(src, dst, l_in.at[n])
        for n, (src, dst) in enumerate(
            ((chosen_hbm, chosen_ref), (k_hbm, k_ref), (v_hbm, v_ref), (q_hbm, q_ref), (router_hbm, router_ref))
        )
    ]
    for load in loads:
        load.start()

    barrier = pltpu.get_barrier_semaphore()

    def greet(ctx_to, y_to):
        pl.semaphore_signal(barrier, inc=1, device_id=(ctx_to, y_to), device_id_type=MESH)

    def greet_chip(r, carry):
        chip_to = (chip + r) % CHIPS
        greet(ctx_of(chip_to, core), y)
        greet(ctx_of(chip_to, 1 - core), y)
        return carry

    lax.fori_loop(1, CHIPS, greet_chip, 0)
    greet(sibling, y)
    for step in range(1, 4):
        greet(ctx, (y + step) % 4)
    even_far, odd_far = z_partners()
    even_far -= {1}
    odd_far -= {-1}
    for delta in sorted(even_far & odd_far):
        greet(ctx_at(at(delta), core), y)

    @pl.when(half == 0)
    def _():
        for delta in sorted(even_far - odd_far):
            greet(ctx_at(at(delta), core), y)

    @pl.when(half == 1)
    def _():
        for delta in sorted(odd_far - even_far):
            greet(ctx_at(at(delta), core), y)

    w_rows = w_hbm.shape[0]
    w_cols = wbuf.shape[1]
    half_rows = w_rows // 2
    own_w = pltpu.make_async_copy(
        w_hbm.at[:, pl.ds(pl.multiple_of(y * w_cols, w_cols), w_cols)],
        wbuf.at[pl.ds(pl.multiple_of(y * w_rows, w_rows), w_rows), :],
        l_w,
    )
    own_w.start()

    for load in loads[:3]:
        load.wait()

    picks_of = []
    ones = []

    def select(hf, kind, ref):
        picked = jnp.dot(
            picks_of[hf], ref[hf * PIECE : (hf + 1) * PIECE, :], preferred_element_type=F32
        ).astype(BF16)
        for head in range(4):
            sel[hf * 4 + head, kind] = picked[:, head * HD : (head + 1) * HD]

    for hf in range(2):
        piece = ctx if hf == 0 else 255 - ctx
        row = chosen_ref[pl.ds(piece // GROUP, 1), :]
        by_rank, by_token = one_hots(row, piece * PIECE)
        picks = dot_nt(by_rank, by_token)
        ones.append((by_rank, by_token, picks))
        picks_of.append(picks.astype(BF16))
        for kind, ref in ((1 - core, k_ref), (core, v_ref)):
            select(hf, kind, ref)

    pl.semaphore_wait(barrier, 18 + len(even_far) + (len(odd_far) - len(even_far)) * half)

    my_q_rows = pl.ds(pl.multiple_of(chip * MOST, MOST), MOST)

    def first_own(chip_to):
        return pltpu.make_async_remote_copy(
            src_ref=sel.at[chip_to, 1],
            dst_ref=pad_own.at[chip],
            send_sem=s1, recv_sem=r1_own,
            device_id=(ctx_of(chip_to, core), y), device_id_type=MESH,
        )

    def first_query(chip_to):
        return pltpu.make_async_remote_copy(
            src_ref=sel.at[chip_to, 2],
            dst_ref=pad_query.at[chip],
            send_sem=s1, recv_sem=r1_query,
            device_id=(ctx_of(chip_to, core), y), device_id_type=MESH,
        )

    def first_other(chip_to):
        return pltpu.make_async_remote_copy(
            src_ref=sel.at[chip_to, 0],
            dst_ref=pad_other.at[chip],
            send_sem=s1, recv_sem=r1_other,
            device_id=(ctx_of(chip_to, 1 - core), y), device_id_type=MESH,
        )

    trips = [(dz, dx) for dz in range(2) for dx in range(4)][1:]
    for dz, dx in sorted(trips, key=lambda t: -(t[0] + min(t[1], 4 - t[1]))):
        chip_to = (half + dz) % 2 * 4 + (x + dx) % 4
        first_own(chip_to).start()
        first_other(chip_to).start()
    first_other(chip).start()
    pad_own[chip] = sel[chip, 1]
    loads[3].wait()
    for hf in range(2):
        select(hf, 2, q_ref)
    for dz, dx in trips:
        first_query((half + dz) % 2 * 4 + (x + dx) % 4).start()
    pad_query[chip] = sel[chip, 2]
    loads[4].wait()
    for hf, (by_rank, by_token, picks) in enumerate(ones):
        place[hf] = dot_nt(by_token, by_rank).astype(BF16)
        rows = slice(hf * PIECE, (hf + 1) * PIECE)
        rsel[hf * MOST : (hf + 1) * MOST, :] = jnp.sum(
            picks * router_ref[rows].astype(F32).reshape(1, PIECE), axis=1, keepdims=True
        )

    quarter_rows = w_rows // 4
    beside = ctx + 2 - x % 2 * 4

    def weight_rows(y_from, step, x_of):
        if step == 2:
            first_row = y_from * w_rows + (x_of % 2 * 2 + core) * quarter_rows
            return pl.ds(pl.multiple_of(first_row, quarter_rows), quarter_rows)
        return pl.ds(pl.multiple_of(y_from * w_rows + core * half_rows, half_rows), half_rows)

    def weights(step):
        y_to = (y + step) % 4
        return pltpu.make_async_remote_copy(
            src_ref=w_hbm.at[
                weight_rows(0, step, x), pl.ds(pl.multiple_of(y_to * w_cols, w_cols), w_cols)
            ],
            dst_ref=wbuf.at[weight_rows(y, step, x), :],
            send_sem=s_w, recv_sem=r_w.at[step - 1],
            device_id=(ctx, y_to), device_id_type=MESH,
        )

    def pass_on(rows, arrived_by, to, lands_by):
        pltpu.make_async_copy(wbuf.at[rows, :], wbuf.at[rows, :], arrived_by).wait()
        for ctx_to, sem in zip(to, lands_by):
            pltpu.make_async_remote_copy(
                src_ref=wbuf.at[rows, :], dst_ref=wbuf.at[rows, :],
                send_sem=s_wf, recv_sem=sem,
                device_id=(ctx_to, y), device_id_type=MESH,
            ).start()

    def share_weights():
        rows = weight_rows((y + 2) % 4, 2, x)
        pass_on(rows, r_w.at[1], (beside, sibling), (r_w.at[3], r_wf))

    def finish_weights():
        pass_on(weight_rows((y + 3) % 4, 1, x), r_w.at[0], (sibling,), (r_wf,))
        pass_on(weight_rows((y + 1) % 4, 3, x), r_w.at[2], (sibling,), (r_wf,))
        pass_on(weight_rows((y + 2) % 4, 2, x + 1), r_w.at[3], (sibling,), (r_wf,))

    for step in (2, 1, 3):
        weights(step).start()

    row = chosen_ref[pl.ds(block, 1), :]
    diagonal = lax.broadcasted_iota(jnp.int32, (PICK, PICK), 0) == lax.broadcasted_iota(
        jnp.int32, (PICK, PICK), 1
    )
    column = jnp.sum(jnp.where(diagonal, row, 0), axis=1, keepdims=True)

    def base_of(device):
        return block * 2048 + (half * 15 + (1 - 2 * half) * device) * PIECE

    slot = lax.broadcasted_iota(jnp.int32, (1, GROUP * MOST), 1)
    slot_core = (core + slot // (CHIPS * MOST)) % 2
    base = base_of(slot // MOST % CHIPS * 2 + slot_core)
    first = jnp.sum((column < base).astype(jnp.int32), axis=0, keepdims=True)
    inside = (column >= base) & (column < base + PIECE)
    entry = lax.broadcasted_iota(jnp.int32, (PICK, GROUP * MOST), 0)
    pick[...] = ((entry - first == slot % MOST) & inside).astype(F32).astype(BF16)
    q_place = (first + slot % MOST)[:, : CHIPS * MOST]

    arrived = pad_own.at[pl.ds(0, CHIPS - 1)]
    pltpu.make_async_copy(arrived, arrived, r1_own).wait()
    pltpu.make_async_copy(pad_other, pad_other, r1_other).wait()

    def rows_of(kind, z_from):
        return pl.ds(pl.multiple_of((kind * RING + z_from) * PICK, PICK), PICK)

    own_side = jnp.dot(
        pick[:, : CHIPS * MOST],
        pad_own[...].reshape(CHIPS * MOST, HD),
        preferred_element_type=F32,
    )
    other_side = jnp.dot(
        pick[:, CHIPS * MOST :],
        pad_other[...].reshape(CHIPS * MOST, HD),
        preferred_element_type=F32,
    )
    block_rows = own_side + other_side
    top_rows, low_rows = block_rows[:HD], block_rows[HD:]

    @pl.when(core == 0)
    def _():
        kv[rows_of(core, z), :] = block_rows.astype(BF16)

    @pl.when(core == 1)
    def _():
        kv[rows_of(core, z), :] = jnp.concatenate([top_rows.T, low_rows.T], axis=0).astype(BF16)


    ways = ((0, 1), (1, -1))
    sent_rows = []

    def rows_of_sub(z_from, sub):
        return pl.ds(pl.multiple_of((core * RING + z_from) * PICK + sub * SUB, SUB), SUB)

    def arrival(side, offset, sub):
        return r2.at[(side * 8 + offset - 1) * SUBS + sub]

    def send(pred, z_from, sub, delta, side, offset):
        rows = rows_of_sub(z_from, sub)
        copy = pltpu.make_async_remote_copy(
            src_ref=kv.at[rows, :], dst_ref=kv.at[rows, :],
            send_sem=s2.at[len(sent_rows)], recv_sem=arrival(side, offset, sub),
            device_id=(ctx_at(at(delta), core), y), device_id_type=MESH,
        )
        sent_rows.append((pred, copy))

        @pl.when(pred)
        def _():
            copy.start()

    def comes(stops, z_from, side, offset, sub):
        if offset == 8 and side != sub * 2 // SUBS:
            return False
        is_wanted = needs((z_from + RING + ways[side][1] * offset) % RING, z_from)
        for stop, before in stops.items():
            if before == offset:
                further = comes(stops, z_from, side, stop, sub)
                if further is not False:
                    is_wanted = is_wanted | further
        return is_wanted

    def send_on(is_mine, stops, z_from, offset, side, sub):
        for stop, before in stops.items():
            if before == offset:
                goes = comes(stops, z_from, side, stop, sub)
                if goes is not False:
                    send(is_mine & goes, z_from, sub, ways[side][1] * (stop - offset), side, stop)

    def receive(offset):
        cases = [(half == 1, EARLY)] if offset % 2 else [(half == 0, EARLY), (half == 1, LATE)]
        for sub in range(SUBS):
            for side, way in ways:
                z_from = at(-way * offset)
                came = False
                for is_mine, stops in cases:
                    here = comes(stops, z_from, side, offset, sub)
                    if here is not False:
                        came = (is_mine & here) if came is False else came | (is_mine & here)
                if came is False:
                    continue

                @pl.when(came)
                def _():
                    rows = rows_of_sub(z_from, sub)
                    pltpu.make_async_copy(
                        kv.at[rows, :], kv.at[rows, :], arrival(side, offset, sub)
                    ).wait()

                for is_mine, stops in cases:
                    send_on(is_mine, stops, z_from, offset, side, sub)

                @pl.when(came & needs(z, z_from))
                def _():
                    to_sibling(z_from, rows_of_sub(z_from, sub)).start()

    def to_sibling(z_from, rows=None):
        rows = rows_of(core, z_from) if rows is None else rows
        return pltpu.make_async_remote_copy(
            src_ref=kv.at[rows, :], dst_ref=kv.at[rows, :],
            send_sem=s_sib.at[z_from], recv_sem=r_sib.at[z_from],
            device_id=(sibling, y), device_id_type=MESH,
        )

    for sub in range(SUBS):
        for side, way in ways:
            send_on(half == 0, EARLY, z, 0, side, sub)
            send_on(half == 1, LATE, z, 0, side, sub)
    to_sibling(z).start()

    pltpu.make_async_copy(arrived, arrived, r1_query).wait()

    scale = HD**-0.5 * 1.4426950408889634

    def from_sibling(z_from):
        rows = rows_of(1 - core, z_from)
        pltpu.make_async_copy(kv.at[rows, :], kv.at[rows, :], r_sib.at[z_from]).wait()


    def scores_of(z_from):
        return dot_nt(kv[rows_of(0, z_from), :], pad_query[...].reshape(CHIPS * MOST, HD)) * scale

    def summed(weight, z_from):
        values = kv[rows_of(1, z_from), :]
        weight = weight.astype(BF16)
        return jnp.dot(values[:HD], weight[:HD], preferred_element_type=F32) + jnp.dot(
            values[HD:], weight[HD:], preferred_element_type=F32
        )

    def attend_own():
        from_sibling(z)
        seen = lax.broadcasted_iota(jnp.int32, (PICK, PICK), 0) <= q_place
        scores = jnp.where(seen, scores_of(z), -1e30)
        top_now = jnp.max(scores, axis=0, keepdims=True)
        weight = jnp.exp2(scores - top_now)
        top[...] = top_now
        total[...] = jnp.sum(weight, axis=0, keepdims=True)
        acc[...] = summed(weight, z)

    def attend_these(z_froms):
        scores = [scores_of(z_from) for z_from in z_froms]
        top_was = top[...]
        top_now = top_was
        for part in scores:
            top_now = jnp.maximum(top_now, jnp.max(part, axis=0, keepdims=True))
        fade = jnp.exp2(top_was - top_now)
        total_now = total[...] * fade
        acc_now = acc[...] * fade
        for part, z_from in zip(scores, z_froms):
            weight = jnp.exp2(part - top_now)
            total_now += jnp.sum(weight, axis=0, keepdims=True)
            acc_now += summed(weight, z_from)
        top[...] = top_now
        total[...] = total_now
        acc[...] = acc_now

    def attend(z_from):
        @pl.when(needs(z, z_from))
        def _():
            from_sibling(z_from)
            attend_these([z_from])

    def attend_both(offset):
        left, right = at(-offset), at(offset)
        wants_left, wants_right = needs(z, left), needs(z, right)

        @pl.when(wants_left)
        def _():
            from_sibling(left)

        @pl.when(wants_right)
        def _():
            from_sibling(right)

        @pl.when(wants_left & wants_right)
        def _():
            attend_these([left, right])

        @pl.when(wants_left != wants_right)
        def _():
            attend_these([lax.select(wants_left, left, right)])

    for step in ORDER:
        if step == "own":
            attend_own()
        elif step == "share":
            share_weights()
        elif step < 0:
            receive(-step)
        elif step == 8:
            attend(at(8))
        else:
            attend_both(step)

    osend[...] = (acc[...] / total[...]).T.astype(BF16)

    att_rows = pl.ds(pl.multiple_of(half * MOST, MOST), MOST)
    att_cols = pl.ds(pl.multiple_of((y * 4 + x) * HD, HD), HD)

    def back(chip_to, y_to):
        return pltpu.make_async_remote_copy(
            src_ref=osend.at[pl.ds(pl.multiple_of(chip_to * MOST, MOST), MOST), :],
            dst_ref=att.at[att_rows, att_cols],
            send_sem=s3, recv_sem=r3,
            device_id=(ctx_of(chip_to, core), y_to), device_id_type=MESH,
        )

    def steps(there):
        return min(there, 4 - there)

    trips = [(dz, dx, dy) for dz in range(2) for dx in range(4) for dy in range(4)][1:]
    for dz, dx, dy in sorted(trips, key=lambda t: -(t[0] + steps(t[1]) + steps(t[2]))):
        back((half + dz) % 2 * 4 + (x + dx) % 4, (y + dy) % 4).start()
    att[att_rows, att_cols] = osend[my_q_rows, :]

    finish_weights()
    own_w.wait()
    three = wbuf.at[pl.ds(0, 3 * half_rows), :]
    pltpu.make_async_copy(three, three, r_wf).wait()
    pltpu.make_async_copy(kv.at[pl.ds(0, 31 * MOST), :], kv.at[pl.ds(0, 31 * MOST), :], r3).wait()

    updates = jnp.dot(att[...], wbuf[...], preferred_element_type=F32) * rsel[...]
    updates = updates.astype(BF16)
    for hf in range(2):
        out_ref[hf * PIECE : (hf + 1) * PIECE, :] = jnp.dot(
            place[hf], updates[hf * MOST : (hf + 1) * MOST, :], preferred_element_type=F32
        ).astype(BF16)

    pltpu.make_async_copy(arrived, arrived, s1).wait()
    pltpu.make_async_copy(arrived, arrived, s1).wait()
    pltpu.make_async_copy(pad_other, pad_other, s1).wait()
    for pred, copy in sent_rows:

        @pl.when(pred)
        def _():
            copy.wait_send()

    def sibling_sent(z_from, carry):
        @pl.when(needs(z, z_from) | (z_from == z))
        def _():
            to_sibling(z_from).wait_send()

        return carry

    lax.fori_loop(0, RING, sibling_sent, 0)
    sent = kv.at[pl.ds(0, 31 * MOST), :]
    pltpu.make_async_copy(sent, sent, s3).wait()
    for rows, sem in ((5 * quarter_rows, s_w), (7 * quarter_rows, s_wf)):
        sent = wbuf.at[pl.ds(0, rows), :]
        pltpu.make_async_copy(sent, sent, sem).wait()


def shards(queries, key_proj, value_proj, router, chosen, out_weight):
    tok_rows = queries.shape[0]
    w_cols = out_weight.shape[1] // 4
    dma = pltpu.SemaphoreType.DMA
    vmem = pl.BlockSpec(memory_space=pltpu.VMEM)
    hbm = pl.BlockSpec(memory_space=pltpu.HBM)
    return pl.pallas_call(
        body,
        out_shape=jax.ShapeDtypeStruct((tok_rows, w_cols), BF16),
        in_specs=[hbm] * 6,
        out_specs=vmem,
        scratch_shapes=[
            pltpu.VMEM(queries.shape, BF16),
            pltpu.VMEM(key_proj.shape, BF16),
            pltpu.VMEM(value_proj.shape, BF16),
            pltpu.VMEM(router.shape, BF16),
            pltpu.VMEM(chosen.shape, jnp.int32),
            dma((5,)),
            pltpu.VMEM((CHIPS, 3, MOST, HD), BF16),
            *[pltpu.VMEM((CHIPS, MOST, HD), BF16)] * 3,
            pltpu.VMEM((2 * RING * PICK, HD), BF16),
            pltpu.VMEM((2 * MOST, 16 * HD), BF16),
            pltpu.VMEM((CHIPS * MOST, HD), BF16),
            pltpu.VMEM((4 * out_weight.shape[0], w_cols), BF16),
            pltpu.VMEM((2, PIECE, MOST), BF16),
            pltpu.VMEM((2 * MOST, 1), F32),
            pltpu.VMEM((1, CHIPS * MOST), F32),
            pltpu.VMEM((1, CHIPS * MOST), F32),
            pltpu.VMEM((HD, CHIPS * MOST), F32),
            pltpu.VMEM((PICK, GROUP * MOST), BF16),
            dma, dma, dma, dma,
            dma((64,)), dma((16 * SUBS,)),
            dma((RING,)), dma((RING,)),
            dma, dma,
            dma, dma((4,)), dma, dma, dma,
        ],
        compiler_params=pltpu.CompilerParams(
            collective_id=0, has_side_effects=True, vmem_limit_bytes=60 * 1024 * 1024
        ),
        name="routed_attention",
    )(queries, key_proj, value_proj, router, chosen, out_weight)


def solution(mesh):
    placed = (P("ctx", "tp"), P("ctx", "tp"), P("ctx", "tp"), P("ctx"), P(), P("tp", None))
    return jax.shard_map(
        shards, mesh=mesh, in_specs=placed, out_specs=P("ctx", "tp"), check_vma=False
    )
```

```python
import functools
import jax
import jax.numpy as jnp
from jax import lax
from jax.experimental import pallas as pl
from jax.experimental.pallas import tpu as pltpu
from jax.sharding import PartitionSpec as P

HD = 128
PIECE = 128
MOST = 32
PICK = 256
GROUP = 16
CHIPS = 8
RING = 16
SUBS = 2
SUB = PICK // SUBS
EARLY = {1: 0, 3: 1, 2: 1, 5: 3, 4: 3, 7: 5, 6: 5, 8: 7}
LATE = {2: 0, 4: 2, 6: 4, 8: 6}
ORDER = (-1, -2, "own", -3, -4, 1, 2, -5, -6, "share", 3, 4, -7, -8, 5, 6, 7, 8)
MESH = pl.DeviceIdType.MESH
F32 = jnp.float32
BF16 = jnp.bfloat16


def z_partners():
    found = (set(), set())
    for source, stops in ((0, EARLY), (1, LATE)):
        for stop, before in stops.items():
            for way in (1, -1):
                found[(source + before) % 2].add(way * (stop - before))
                found[(source + stop) % 2].add(way * (before - stop))
    return found


def one_hots(chosen_row, base):
    first = jnp.sum((chosen_row < base).astype(jnp.int32), axis=1, keepdims=True)
    inside = (chosen_row >= base) & (chosen_row < base + PIECE)
    entry = lax.broadcasted_iota(jnp.int32, (MOST, PICK), 1)
    rank = lax.broadcasted_iota(jnp.int32, (MOST, PICK), 0)
    by_rank = (entry - first == rank) & inside
    token = lax.broadcasted_iota(jnp.int32, (PIECE, PICK), 0)
    by_token = chosen_row - base == token
    return by_rank.astype(F32).astype(BF16), by_token.astype(F32).astype(BF16)


def dot_nt(a, b):
    return lax.dot_general(a, b, (((1,), (1,)), ((), ())), preferred_element_type=F32)


def body(
    q_hbm, k_hbm, v_hbm, router_hbm, chosen_hbm, w_hbm, out_ref,
    q_ref, k_ref, v_ref, router_ref, chosen_ref, l_in, sel, pad_own, pad_other, pad_query, kv, att, osend, wbuf, place, rsel, top, total, acc, pick,
    s1, r1_own, r1_other, r1_query, s2, r2, s_sib, r_sib, s3, r3, s_w, r_w, s_wf, r_wf, l_w,
):
    ctx = lax.axis_index("ctx")
    y = lax.axis_index("tp")
    z = ctx // 8
    core = ctx % 2
    x = (ctx // 2) % 4
    group = ctx // GROUP
    chip = (ctx // 2) % CHIPS
    half = z % 2

    def ctx_of(chip_to, core_to):
        return group * GROUP + chip_to * 2 + core_to

    def ctx_at(z_to, core_to):
        return z_to * 8 + x * 2 + core_to

    sibling = ctx_of(chip, 1 - core)

    def at(delta):
        return (z + RING + delta) % RING

    def block_at(z_of):
        return z_of % 2 * (15 - z_of // 2 * 2) + z_of // 2

    def needs(z_to, z_from):
        return block_at(z_from) < block_at(z_to)

    block = block_at(z)
    loads = [
        pltpu.make_async_copy(src, dst, l_in.at[n])
        for n, (src, dst) in enumerate(
            ((chosen_hbm, chosen_ref), (k_hbm, k_ref), (v_hbm, v_ref), (q_hbm, q_ref), (router_hbm, router_ref))
        )
    ]
    for load in loads:
        load.start()

    barrier = pltpu.get_barrier_semaphore()

    def greet(ctx_to, y_to):
        pl.semaphore_signal(barrier, inc=1, device_id=(ctx_to, y_to), device_id_type=MESH)

    def greet_chip(r, carry):
        chip_to = (chip + r) % CHIPS
        greet(ctx_of(chip_to, core), y)
        greet(ctx_of(chip_to, 1 - core), y)
        return carry

    lax.fori_loop(1, CHIPS, greet_chip, 0)
    greet(sibling, y)
    for step in range(1, 4):
        greet(ctx, (y + step) % 4)
    even_far, odd_far = z_partners()
    even_far -= {1}
    odd_far -= {-1}
    for delta in sorted(even_far & odd_far):
        greet(ctx_at(at(delta), core), y)

    @pl.when(half == 0)
    def _():
        for delta in sorted(even_far - odd_far):
            greet(ctx_at(at(delta), core), y)

    @pl.when(half == 1)
    def _():
        for delta in sorted(odd_far - even_far):
            greet(ctx_at(at(delta), core), y)

    w_rows = w_hbm.shape[0]
    w_cols = wbuf.shape[1]
    half_rows = w_rows // 2
    own_w = pltpu.make_async_copy(
        w_hbm.at[:, pl.ds(pl.multiple_of(y * w_cols, w_cols), w_cols)],
        wbuf.at[pl.ds(pl.multiple_of(y * w_rows, w_rows), w_rows), :],
        l_w,
    )
    own_w.start()

    for load in loads[:3]:
        load.wait()

    picks_of = []
    ones = []

    def select(hf, kind, ref):
        picked = jnp.dot(
            picks_of[hf], ref[hf * PIECE : (hf + 1) * PIECE, :], preferred_element_type=F32
        ).astype(BF16)
        for head in range(4):
            sel[hf * 4 + head, kind] = picked[:, head * HD : (head + 1) * HD]

    for hf in range(2):
        piece = ctx if hf == 0 else 255 - ctx
        row = chosen_ref[pl.ds(piece // GROUP, 1), :]
        by_rank, by_token = one_hots(row, piece * PIECE)
        picks = dot_nt(by_rank, by_token)
        ones.append((by_rank, by_token, picks))
        picks_of.append(picks.astype(BF16))
        for kind, ref in ((1 - core, k_ref), (core, v_ref)):
            select(hf, kind, ref)

    pl.semaphore_wait(barrier, 18 + len(even_far) + (len(odd_far) - len(even_far)) * half)

    my_q_rows = pl.ds(pl.multiple_of(chip * MOST, MOST), MOST)

    def first_own(chip_to):
        return pltpu.make_async_remote_copy(
            src_ref=sel.at[chip_to, 1],
            dst_ref=pad_own.at[chip],
            send_sem=s1, recv_sem=r1_own,
            device_id=(ctx_of(chip_to, core), y), device_id_type=MESH,
        )

    def first_query(chip_to):
        return pltpu.make_async_remote_copy(
            src_ref=sel.at[chip_to, 2],
            dst_ref=pad_query.at[chip],
            send_sem=s1, recv_sem=r1_query,
            device_id=(ctx_of(chip_to, core), y), device_id_type=MESH,
        )

    def first_other(chip_to):
        return pltpu.make_async_remote_copy(
            src_ref=sel.at[chip_to, 0],
            dst_ref=pad_other.at[chip],
            send_sem=s1, recv_sem=r1_other,
            device_id=(ctx_of(chip_to, 1 - core), y), device_id_type=MESH,
        )

    trips = [(dz, dx) for dz in range(2) for dx in range(4)][1:]
    for dz, dx in sorted(trips, key=lambda t: -(t[0] + min(t[1], 4 - t[1]))):
        chip_to = (half + dz) % 2 * 4 + (x + dx) % 4
        first_own(chip_to).start()
        first_other(chip_to).start()
    first_other(chip).start()
    pad_own[chip] = sel[chip, 1]
    loads[3].wait()
    for hf in range(2):
        select(hf, 2, q_ref)
    for dz, dx in trips:
        first_query((half + dz) % 2 * 4 + (x + dx) % 4).start()
    pad_query[chip] = sel[chip, 2]
    loads[4].wait()
    for hf, (by_rank, by_token, picks) in enumerate(ones):
        place[hf] = dot_nt(by_token, by_rank).astype(BF16)
        rows = slice(hf * PIECE, (hf + 1) * PIECE)
        rsel[hf * MOST : (hf + 1) * MOST, :] = jnp.sum(
            picks * router_ref[rows].astype(F32).reshape(1, PIECE), axis=1, keepdims=True
        )

    quarter_rows = w_rows // 4
    beside = ctx + 2 - x % 2 * 4

    def weight_rows(y_from, step, x_of):
        if step == 2:
            first_row = y_from * w_rows + (x_of % 2 * 2 + core) * quarter_rows
            return pl.ds(pl.multiple_of(first_row, quarter_rows), quarter_rows)
        return pl.ds(pl.multiple_of(y_from * w_rows + core * half_rows, half_rows), half_rows)

    def weights(step):
        y_to = (y + step) % 4
        return pltpu.make_async_remote_copy(
            src_ref=w_hbm.at[
                weight_rows(0, step, x), pl.ds(pl.multiple_of(y_to * w_cols, w_cols), w_cols)
            ],
            dst_ref=wbuf.at[weight_rows(y, step, x), :],
            send_sem=s_w, recv_sem=r_w.at[step - 1],
            device_id=(ctx, y_to), device_id_type=MESH,
        )

    def pass_on(rows, arrived_by, to, lands_by):
        pltpu.make_async_copy(wbuf.at[rows, :], wbuf.at[rows, :], arrived_by).wait()
        for ctx_to, sem in zip(to, lands_by):
            pltpu.make_async_remote_copy(
                src_ref=wbuf.at[rows, :], dst_ref=wbuf.at[rows, :],
                send_sem=s_wf, recv_sem=sem,
                device_id=(ctx_to, y), device_id_type=MESH,
            ).start()

    def share_weights():
        rows = weight_rows((y + 2) % 4, 2, x)
        pass_on(rows, r_w.at[1], (beside, sibling), (r_w.at[3], r_wf))

    def finish_weights():
        pass_on(weight_rows((y + 3) % 4, 1, x), r_w.at[0], (sibling,), (r_wf,))
        pass_on(weight_rows((y + 1) % 4, 3, x), r_w.at[2], (sibling,), (r_wf,))
        pass_on(weight_rows((y + 2) % 4, 2, x + 1), r_w.at[3], (sibling,), (r_wf,))

    for step in (2, 1, 3):
        weights(step).start()

    row = chosen_ref[pl.ds(block, 1), :]
    diagonal = lax.broadcasted_iota(jnp.int32, (PICK, PICK), 0) == lax.broadcasted_iota(
        jnp.int32, (PICK, PICK), 1
    )
    column = jnp.sum(jnp.where(diagonal, row, 0), axis=1, keepdims=True)

    def base_of(device):
        return block * 2048 + (half * 15 + (1 - 2 * half) * device) * PIECE

    slot = lax.broadcasted_iota(jnp.int32, (1, GROUP * MOST), 1)
    slot_core = (core + slot // (CHIPS * MOST)) % 2
    base = base_of(slot // MOST % CHIPS * 2 + slot_core)
    first = jnp.sum((column < base).astype(jnp.int32), axis=0, keepdims=True)
    inside = (column >= base) & (column < base + PIECE)
    entry = lax.broadcasted_iota(jnp.int32, (PICK, GROUP * MOST), 0)
    pick[...] = ((entry - first == slot % MOST) & inside).astype(F32).astype(BF16)
    q_place = (first + slot % MOST)[:, : CHIPS * MOST]

    arrived = pad_own.at[pl.ds(0, CHIPS - 1)]
    pltpu.make_async_copy(arrived, arrived, r1_own).wait()
    pltpu.make_async_copy(pad_other, pad_other, r1_other).wait()

    def rows_of(kind, z_from):
        return pl.ds(pl.multiple_of((kind * RING + z_from) * PICK, PICK), PICK)

    own_side = jnp.dot(
        pick[:, : CHIPS * MOST],
        pad_own[...].reshape(CHIPS * MOST, HD),
        preferred_element_type=F32,
    )
    other_side = jnp.dot(
        pick[:, CHIPS * MOST :],
        pad_other[...].reshape(CHIPS * MOST, HD),
        preferred_element_type=F32,
    )
    block_rows = own_side + other_side
    top_rows, low_rows = block_rows[:HD], block_rows[HD:]

    @pl.when(core == 0)
    def _():
        kv[rows_of(core, z), :] = block_rows.astype(BF16)

    @pl.when(core == 1)
    def _():
        kv[rows_of(core, z), :] = jnp.concatenate([top_rows.T, low_rows.T], axis=0).astype(BF16)


    ways = ((0, 1), (1, -1))
    sent_rows = []

    def rows_of_sub(z_from, sub):
        return pl.ds(pl.multiple_of((core * RING + z_from) * PICK + sub * SUB, SUB), SUB)

    def arrival(side, offset, sub):
        return r2.at[(side * 8 + offset - 1) * SUBS + sub]

    def send(pred, z_from, sub, delta, side, offset):
        rows = rows_of_sub(z_from, sub)
        copy = pltpu.make_async_remote_copy(
            src_ref=kv.at[rows, :], dst_ref=kv.at[rows, :],
            send_sem=s2.at[len(sent_rows)], recv_sem=arrival(side, offset, sub),
            device_id=(ctx_at(at(delta), core), y), device_id_type=MESH,
        )
        sent_rows.append((pred, copy))

        @pl.when(pred)
        def _():
            copy.start()

    def comes(stops, z_from, side, offset, sub):
        if offset == 8 and side != sub * 2 // SUBS:
            return False
        is_wanted = needs((z_from + RING + ways[side][1] * offset) % RING, z_from)
        for stop, before in stops.items():
            if before == offset:
                further = comes(stops, z_from, side, stop, sub)
                if further is not False:
                    is_wanted = is_wanted | further
        return is_wanted

    def send_on(is_mine, stops, z_from, offset, side, sub):
        for stop, before in stops.items():
            if before == offset:
                goes = comes(stops, z_from, side, stop, sub)
                if goes is not False:
                    send(is_mine & goes, z_from, sub, ways[side][1] * (stop - offset), side, stop)

    def receive(offset):
        cases = [(half == 1, EARLY)] if offset % 2 else [(half == 0, EARLY), (half == 1, LATE)]
        for sub in range(SUBS):
            for side, way in ways:
                z_from = at(-way * offset)
                came = False
                for is_mine, stops in cases:
                    here = comes(stops, z_from, side, offset, sub)
                    if here is not False:
                        came = (is_mine & here) if came is False else came | (is_mine & here)
                if came is False:
                    continue

                @pl.when(came)
                def _():
                    rows = rows_of_sub(z_from, sub)
                    pltpu.make_async_copy(
                        kv.at[rows, :], kv.at[rows, :], arrival(side, offset, sub)
                    ).wait()

                for is_mine, stops in cases:
                    send_on(is_mine, stops, z_from, offset, side, sub)

                @pl.when(came & needs(z, z_from))
                def _():
                    to_sibling(z_from, rows_of_sub(z_from, sub)).start()

    def to_sibling(z_from, rows=None):
        rows = rows_of(core, z_from) if rows is None else rows
        return pltpu.make_async_remote_copy(
            src_ref=kv.at[rows, :], dst_ref=kv.at[rows, :],
            send_sem=s_sib.at[z_from], recv_sem=r_sib.at[z_from],
            device_id=(sibling, y), device_id_type=MESH,
        )

    for sub in range(SUBS):
        for side, way in ways:
            send_on(half == 0, EARLY, z, 0, side, sub)
            send_on(half == 1, LATE, z, 0, side, sub)
    to_sibling(z).start()

    pltpu.make_async_copy(arrived, arrived, r1_query).wait()

    scale = HD**-0.5 * 1.4426950408889634

    def from_sibling(z_from):
        rows = rows_of(1 - core, z_from)
        pltpu.make_async_copy(kv.at[rows, :], kv.at[rows, :], r_sib.at[z_from]).wait()


    def scores_of(z_from):
        return dot_nt(kv[rows_of(0, z_from), :], pad_query[...].reshape(CHIPS * MOST, HD)) * scale

    def summed(weight, z_from):
        values = kv[rows_of(1, z_from), :]
        weight = weight.astype(BF16)
        return jnp.dot(values[:HD], weight[:HD], preferred_element_type=F32) + jnp.dot(
            values[HD:], weight[HD:], preferred_element_type=F32
        )

    def attend_own():
        from_sibling(z)
        seen = lax.broadcasted_iota(jnp.int32, (PICK, PICK), 0) <= q_place
        scores = jnp.where(seen, scores_of(z), -1e30)
        top_now = jnp.max(scores, axis=0, keepdims=True)
        weight = jnp.exp2(scores - top_now)
        top[...] = top_now
        total[...] = jnp.sum(weight, axis=0, keepdims=True)
        acc[...] = summed(weight, z)

    def attend_these(z_froms):
        scores = [scores_of(z_from) for z_from in z_froms]
        top_was = top[...]
        top_now = top_was
        for part in scores:
            top_now = jnp.maximum(top_now, jnp.max(part, axis=0, keepdims=True))
        fade = jnp.exp2(top_was - top_now)
        total_now = total[...] * fade
        acc_now = acc[...] * fade
        for part, z_from in zip(scores, z_froms):
            weight = jnp.exp2(part - top_now)
            total_now += jnp.sum(weight, axis=0, keepdims=True)
            acc_now += summed(weight, z_from)
        top[...] = top_now
        total[...] = total_now
        acc[...] = acc_now

    def attend(z_from):
        @pl.when(needs(z, z_from))
        def _():
            from_sibling(z_from)
            attend_these([z_from])

    def attend_both(offset):
        left, right = at(-offset), at(offset)
        wants_left, wants_right = needs(z, left), needs(z, right)

        @pl.when(wants_left)
        def _():
            from_sibling(left)

        @pl.when(wants_right)
        def _():
            from_sibling(right)

        @pl.when(wants_left & wants_right)
        def _():
            attend_these([left, right])

        @pl.when(wants_left != wants_right)
        def _():
            attend_these([lax.select(wants_left, left, right)])

    for step in ORDER:
        if step == "own":
            attend_own()
        elif step == "share":
            share_weights()
        elif step < 0:
            receive(-step)
        elif step == 8:
            attend(at(8))
        else:
            attend_both(step)

    osend[...] = (acc[...] / total[...]).T.astype(BF16)

    att_rows = pl.ds(pl.multiple_of(half * MOST, MOST), MOST)
    att_cols = pl.ds(pl.multiple_of((y * 4 + x) * HD, HD), HD)

    def back(chip_to, y_to):
        return pltpu.make_async_remote_copy(
            src_ref=osend.at[pl.ds(pl.multiple_of(chip_to * MOST, MOST), MOST), :],
            dst_ref=att.at[att_rows, att_cols],
            send_sem=s3, recv_sem=r3,
            device_id=(ctx_of(chip_to, core), y_to), device_id_type=MESH,
        )

    def steps(there):
        return min(there, 4 - there)

    trips = [(dz, dx, dy) for dz in range(2) for dx in range(4) for dy in range(4)][1:]
    for dz, dx, dy in sorted(trips, key=lambda t: -(t[0] + steps(t[1]) + steps(t[2]))):
        back((half + dz) % 2 * 4 + (x + dx) % 4, (y + dy) % 4).start()
    att[att_rows, att_cols] = osend[my_q_rows, :]

    finish_weights()
    own_w.wait()
    three = wbuf.at[pl.ds(0, 3 * half_rows), :]
    pltpu.make_async_copy(three, three, r_wf).wait()
    pltpu.make_async_copy(kv.at[pl.ds(0, 31 * MOST), :], kv.at[pl.ds(0, 31 * MOST), :], r3).wait()

    updates = jnp.dot(att[...], wbuf[...], preferred_element_type=F32) * rsel[...]
    updates = updates.astype(BF16)
    for hf in range(2):
        out_ref[hf * PIECE : (hf + 1) * PIECE, :] = jnp.dot(
            place[hf], updates[hf * MOST : (hf + 1) * MOST, :], preferred_element_type=F32
        ).astype(BF16)

    pltpu.make_async_copy(arrived, arrived, s1).wait()
    pltpu.make_async_copy(arrived, arrived, s1).wait()
    pltpu.make_async_copy(pad_other, pad_other, s1).wait()
    for pred, copy in sent_rows:

        @pl.when(pred)
        def _():
            copy.wait_send()

    def sibling_sent(z_from, carry):
        @pl.when(needs(z, z_from) | (z_from == z))
        def _():
            to_sibling(z_from).wait_send()

        return carry

    lax.fori_loop(0, RING, sibling_sent, 0)
    sent = kv.at[pl.ds(0, 31 * MOST), :]
    pltpu.make_async_copy(sent, sent, s3).wait()
    for rows, sem in ((5 * quarter_rows, s_w), (7 * quarter_rows, s_wf)):
        sent = wbuf.at[pl.ds(0, rows), :]
        pltpu.make_async_copy(sent, sent, sem).wait()


def shards(queries, key_proj, value_proj, router, chosen, out_weight):
    tok_rows = queries.shape[0]
    w_cols = out_weight.shape[1] // 4
    dma = pltpu.SemaphoreType.DMA
    vmem = pl.BlockSpec(memory_space=pltpu.VMEM)
    hbm = pl.BlockSpec(memory_space=pltpu.HBM)
    return pl.pallas_call(
        body,
        out_shape=jax.ShapeDtypeStruct((tok_rows, w_cols), BF16),
        in_specs=[hbm] * 6,
        out_specs=vmem,
        scratch_shapes=[
            pltpu.VMEM(queries.shape, BF16),
            pltpu.VMEM(key_proj.shape, BF16),
            pltpu.VMEM(value_proj.shape, BF16),
            pltpu.VMEM(router.shape, BF16),
            pltpu.VMEM(chosen.shape, jnp.int32),
            dma((5,)),
            pltpu.VMEM((CHIPS, 3, MOST, HD), BF16),
            *[pltpu.VMEM((CHIPS, MOST, HD), BF16)] * 3,
            pltpu.VMEM((2 * RING * PICK, HD), BF16),
            pltpu.VMEM((2 * MOST, 16 * HD), BF16),
            pltpu.VMEM((CHIPS * MOST, HD), BF16),
            pltpu.VMEM((4 * out_weight.shape[0], w_cols), BF16),
            pltpu.VMEM((2, PIECE, MOST), BF16),
            pltpu.VMEM((2 * MOST, 1), F32),
            pltpu.VMEM((1, CHIPS * MOST), F32),
            pltpu.VMEM((1, CHIPS * MOST), F32),
            pltpu.VMEM((HD, CHIPS * MOST), F32),
            pltpu.VMEM((PICK, GROUP * MOST), BF16),
            dma, dma, dma, dma,
            dma((64,)), dma((16 * SUBS,)),
            dma((RING,)), dma((RING,)),
            dma, dma,
            dma, dma((4,)), dma, dma, dma,
        ],
        compiler_params=pltpu.CompilerParams(
            collective_id=0, has_side_effects=True, vmem_limit_bytes=60 * 1024 * 1024
        ),
        name="routed_attention",
    )(queries, key_proj, value_proj, router, chosen, out_weight)


def solution(mesh):
    placed = (P("ctx", "tp"), P("ctx", "tp"), P("ctx", "tp"), P("ctx"), P(), P("tp", None))
    return jax.shard_map(
        shards, mesh=mesh, in_specs=placed, out_specs=P("ctx", "tp"), check_vma=False
    )
```
